32 devices in a mesh: slab: 32 (over z, y, x, core), gy: 1.
Axes of the slice: x: 2, y: 2, z: 4, core: 2. Of those that a mesh axis runs over, the one named last changes fastest.
Arguments:
- electrostatic_voltages: float32 [256, 64, 1024], P('slab', 'gy'), may hold values from -6 to 6
- initial_electrons: float32 [256, 64, 1024], P('slab', 'gy'), may hold values from 0.5 to 2
- creation_amounts: float32 [256, 64, 1024], P('slab', 'gy'), may hold values from 0.2 to 5
- annihilation_coefficient: float32 [256, 64, 1024], P('slab', 'gy'), may hold values from 0.5 to 2
- crystal_orientation_class: int32 [256, 64, 1024], P('slab', 'gy'), may hold values from 0 to 3
- crystal_barrier_shift: float32 [4], replicated, may hold values from -1.5 to 1.5
- restrict_matrix_first: float32 [128, 256], replicated, may hold values from 0 to 1, as said below
- restrict_matrix_second: float32 [32, 64], P('gy'), may hold values from 0 to 1, as said below
- restrict_matrix_third: float32 [256, 1024], replicated, may hold values from 0 to 1, as said below
- cooling_coefficient: float32 [256, 32, 128], P('slab', 'gy'), may hold values from 0.05 to 1
- initial_warming: float32 [256, 32, 128], P('slab', 'gy'), may hold values from 0.5 to 1.5
Outputs:
- density_out: float32 [256, 64, 1024], P('slab', 'gy')
- thermal_out: float32 [256, 32, 128], P('slab', 'gy')
- fine_mesh_warming: float32 [256, 64, 1024], P('slab', 'gy')
The draws below stay inside these ranges and needn't reach their ends.
Inputs may be any that keep to these rules, and one draw needn't show every extreme that they name: `restrict_matrix_first`: row a is nonnegative, nonzero at most on columns 2a - 1 to 2a + 2, and sums to 1. `restrict_matrix_second`: row b, with t = b % 32, is nonnegative, nonzero at most on columns 2t - 1 to 2t + 2, and sums to 1. `restrict_matrix_third`: row c is nonnegative, nonzero at most on columns 4c - 2 to 4c + 5, and sums to 1.
All inputs are finite; a program needn't handle non-finite values.
Results may differ from the reference program's by a relative error of at most 0.0003.
Values sent between devices are 32-bit elements; how exact they have to be, the bound alone decides.
A program may use at most 64 MiB of HBM per device.

```python
import math
import jax
import jax.numpy as jnp
from jax import lax

CY = 64
DEVICE_CELLS_Z = 1024
GRAINS = 4
SWEEPS = 2
HEAT_SWEEPS = 3
DEVICE_CELLS_X = 256
DEVICE_CELLS_Y = 64
HOT_MESH_ALONG_I = 128
TYD = 32
HOT_MESH_ALONG_J = 32
HOT_MESH_ALONG_K = 256
N_GY = 1


def banded_rows(key, local_rows, cols, ratio, taps):
    width = len(taps)
    shift = (width - ratio) // 2
    jitter = jax.random.uniform(key, (local_rows.shape[0], width), jnp.float32, 0.5, 1.5)
    column = jnp.arange(cols, dtype=jnp.int32)[None, :]
    start = (ratio * local_rows - shift)[:, None]
    matrix = jnp.zeros((local_rows.shape[0], cols), jnp.float32)
    for offset in range(width):
        matrix = matrix + jnp.where(column == start + offset, taps[offset] * jitter[:, offset:offset + 1], jnp.float32(0.0))
    return matrix / jnp.sum(matrix, axis=1, keepdims=True)


def draw_restrict_matrix_first(key, part):
    rows = jnp.arange(HOT_MESH_ALONG_I, dtype=jnp.int32)
    return banded_rows(jax.random.fold_in(key, 11), rows, DEVICE_CELLS_X, 2, [1.0, 3.0, 3.0, 1.0])


def draw_restrict_matrix_second(key, part):
    rows = jnp.arange(HOT_MESH_ALONG_J, dtype=jnp.int32) % TYD
    return banded_rows(jax.random.fold_in(key, 12), rows, CY, 2, [1.0, 3.0, 3.0, 1.0])


def draw_restrict_matrix_third(key, part):
    rows = jnp.arange(HOT_MESH_ALONG_K, dtype=jnp.int32)
    return banded_rows(jax.random.fold_in(key, 13), rows, DEVICE_CELLS_Z, 4, [1.0, 2.0, 3.0, 4.0, 4.0, 3.0, 2.0, 1.0])


def with_ends(entries, own_key, smallest, top_value):
    dims = entries.shape
    place = [jax.random.randint(jax.random.fold_in(own_key, axis), (), 0, dims[axis]) for axis in range(len(dims))]
    entries = entries.at[tuple(place)].set(smallest)
    longest = dims.index(max(dims))
    place[longest] = (place[longest] + 1) % dims[longest]
    return entries.at[tuple(place)].set(top_value)


def steps_of(stream_key, extent, split, low, high):
    level = 1.0
    for dim, parts in split:
        steps = jax.random.uniform(jax.random.fold_in(jax.random.fold_in(stream_key, 6), dim), (parts,), jnp.float32, low / len(split), high / len(split))
        level = level * jnp.repeat(jnp.exp(steps), extent[dim] // parts).reshape((-1,) + (1,) * (len(extent) - 1 - dim))
    return level


def scatter_about(key, extent, scale, most, split=(), held_as=jnp.bfloat16):
    factor_of = steps_of(key, extent, split, -0.22, 0.18) if split else 1.0
    values = jax.random.normal(key, extent, jnp.float32) * scale * factor_of
    return jnp.minimum(jnp.maximum(values, -most), most).astype(held_as)


def setup_inputs(seed: int = 0) -> dict:
    seeds = jax.random.split(jax.random.key(seed), 12)
    electrostatic_voltages = scatter_about(seeds[0], (DEVICE_CELLS_X, DEVICE_CELLS_Y, DEVICE_CELLS_Z), 1.0, 6.0, ((0, 32),), jnp.float32)
    initial_electrons = jnp.clip(jnp.exp(math.log(2.0) - 1.3862944 * jax.random.uniform(seeds[1], (DEVICE_CELLS_X, DEVICE_CELLS_Y, DEVICE_CELLS_Z), jnp.float32) ** steps_of(seeds[1], (DEVICE_CELLS_X, DEVICE_CELLS_Y, DEVICE_CELLS_Z), ((0, 32),), -0.2, 0.2)), 0.5, 2.0)
    creation_amounts = jnp.clip(jnp.exp(math.log(5.0) - 3.218876 * jax.random.uniform(seeds[2], (DEVICE_CELLS_X, DEVICE_CELLS_Y, DEVICE_CELLS_Z), jnp.float32) ** steps_of(seeds[2], (DEVICE_CELLS_X, DEVICE_CELLS_Y, DEVICE_CELLS_Z), ((0, 32),), -0.2, 0.2)), 0.2, 5.0)
    annihilation_coefficient = jnp.clip(jnp.exp(math.log(2.0) - 1.3862944 * jax.random.uniform(seeds[3], (DEVICE_CELLS_X, DEVICE_CELLS_Y, DEVICE_CELLS_Z), jnp.float32) ** steps_of(seeds[3], (DEVICE_CELLS_X, DEVICE_CELLS_Y, DEVICE_CELLS_Z), ((0, 32),), -0.2, 0.2)), 0.5, 2.0)
    crystal_orientation_class = with_ends(jax.random.randint(seeds[4], (DEVICE_CELLS_X, DEVICE_CELLS_Y, DEVICE_CELLS_Z), 0, GRAINS), jax.random.fold_in(seeds[4], 1), 0, GRAINS - 1).astype(jnp.int32)
    crystal_barrier_shift = jnp.clip(jax.random.uniform(seeds[5], (GRAINS,), jnp.float32, -1.5, 1.5), -1.5, 1.5)
    restrict_matrix_first = draw_restrict_matrix_first(jax.random.fold_in(seeds[11], 71), 0)
    restrict_matrix_second = draw_restrict_matrix_second(jax.random.fold_in(seeds[11], 71), 0)
    restrict_matrix_third = draw_restrict_matrix_third(jax.random.fold_in(seeds[11], 71), 0)
    cooling_coefficient = jnp.clip(jnp.exp(math.log(1.0) - 2.9957323 * jax.random.uniform(seeds[9], (HOT_MESH_ALONG_K, HOT_MESH_ALONG_J, HOT_MESH_ALONG_I), jnp.float32) ** steps_of(seeds[9], (HOT_MESH_ALONG_K, HOT_MESH_ALONG_J, HOT_MESH_ALONG_I), ((0, 32),), -0.2, 0.2)), 0.05, 1.0)
    initial_warming = jnp.clip(0.5 + 1.0 * jax.random.uniform(seeds[10], (HOT_MESH_ALONG_K, HOT_MESH_ALONG_J, HOT_MESH_ALONG_I), jnp.float32) ** steps_of(seeds[10], (HOT_MESH_ALONG_K, HOT_MESH_ALONG_J, HOT_MESH_ALONG_I), ((0, 32),), -0.2, 0.2), 0.5, 1.5)
    return dict(electrostatic_voltages=electrostatic_voltages, initial_electrons=initial_electrons, creation_amounts=creation_amounts, annihilation_coefficient=annihilation_coefficient, crystal_orientation_class=crystal_orientation_class, crystal_barrier_shift=crystal_barrier_shift, restrict_matrix_first=restrict_matrix_first, restrict_matrix_second=restrict_matrix_second, restrict_matrix_third=restrict_matrix_third, cooling_coefficient=cooling_coefficient, initial_warming=initial_warming)


def bernoulli(value):
    small = jnp.abs(value) < 1e-4
    safe = jnp.where(small, jnp.float32(1.0), value)
    return jnp.where(small, 1.0 - 0.5 * value, safe / jnp.expm1(safe))


def neighbour_values(padded):
    return [padded[2:, 1:-1, 1:-1], padded[:-2, 1:-1, 1:-1], padded[1:-1, 2:, 1:-1], padded[1:-1, :-2, 1:-1], padded[1:-1, 1:-1, 2:], padded[1:-1, 1:-1, :-2]]


def reference(electrostatic_voltages, initial_electrons, creation_amounts, annihilation_coefficient, crystal_orientation_class, crystal_barrier_shift, restrict_matrix_first, restrict_matrix_second, restrict_matrix_third, cooling_coefficient, initial_warming):
    upper_limit = lax.Precision.HIGHEST
    effective = electrostatic_voltages
    for grain in range(GRAINS):
        effective = effective + jnp.where(crystal_orientation_class == grain, crystal_barrier_shift[grain], jnp.float32(0.0))
    beside_all = neighbour_values(jnp.pad(effective, 1))
    voltage_gradients = [leftover_portion - effective for leftover_portion in beside_all]
    bernoulli_coefficients = [bernoulli(voltage_gradient) for voltage_gradient in voltage_gradients]
    denominator_quantity = annihilation_coefficient
    for bernoulli_coefficient, voltage_gradient in zip(bernoulli_coefficients, voltage_gradients):
        denominator_quantity = denominator_quantity + (bernoulli_coefficient + voltage_gradient)
    electron_concentration = initial_electrons
    for repeat in range(SWEEPS):
        fraction_top_quantity = creation_amounts
        for bernoulli_coefficient, leftover_portion in zip(bernoulli_coefficients, neighbour_values(jnp.pad(electron_concentration, 1))):
            fraction_top_quantity = fraction_top_quantity + bernoulli_coefficient * leftover_portion
        electron_concentration = fraction_top_quantity / denominator_quantity
    joule_power_input = jnp.zeros_like(electron_concentration)
    for bernoulli_coefficient, voltage_gradient, leftover_portion in zip(bernoulli_coefficients, voltage_gradients, neighbour_values(jnp.pad(electron_concentration, 1))):
        joule_power_input = joule_power_input + voltage_gradient * (bernoulli_coefficient * leftover_portion - (bernoulli_coefficient + voltage_gradient) * electron_concentration)
    joule_power_input = 0.5 * joule_power_input
    y_block_count = restrict_matrix_second.reshape(N_GY, TYD, CY)
    along_y = jnp.einsum('gty,xgyz->xgtz', y_block_count, joule_power_input.reshape(DEVICE_CELLS_X, N_GY, CY, DEVICE_CELLS_Z), precision=upper_limit).reshape(DEVICE_CELLS_X, HOT_MESH_ALONG_J, DEVICE_CELLS_Z)
    along_z = jnp.einsum('cz,xtz->ctx', restrict_matrix_third, along_y, precision=upper_limit)
    source = jnp.einsum('ctx,ax->cta', along_z, restrict_matrix_first, precision=upper_limit)
    warming_distribution = initial_warming
    for repeat in range(HEAT_SWEEPS):
        total = source
        for leftover_portion in neighbour_values(jnp.pad(warming_distribution, 1)):
            total = total + leftover_portion
        warming_distribution = total / (6.0 + cooling_coefficient)
    spread = jnp.einsum('cta,ax->ctx', warming_distribution, restrict_matrix_first, precision=upper_limit)
    raised_field = jnp.einsum('ctx,cz->xtz', spread, restrict_matrix_third, precision=upper_limit).reshape(DEVICE_CELLS_X, N_GY, TYD, DEVICE_CELLS_Z)
    fine_mesh_warming = 16.0 * jnp.einsum('efc,iefk->ieck', y_block_count, raised_field, precision=upper_limit).reshape(DEVICE_CELLS_X, DEVICE_CELLS_Y, DEVICE_CELLS_Z)
    return electron_concentration, warming_distribution, fine_mesh_warming
```

```python
import functools

import jax
import jax.numpy as jnp
from jax import lax
from jax.experimental import pallas as pl
from jax.experimental.pallas import tpu as pltpu
from jax.sharding import PartitionSpec as P

MESH = pl.DeviceIdType.MESH
HIGHEST = lax.Precision.HIGHEST
GRAINS = 4
HEAT_SWEEPS = 3
PAD = 8
MIB = 1024 * 1024


def bernoulli(u):
    small = jnp.abs(u) < 0.03125
    series = 1.0 + u * (u * (1.0 / 12.0) - 0.5)
    return jnp.where(small, series, u / (jnp.exp(u) - 1.0))


def device_kernel(
    slabs, yblocks,
    shift_ref, wx_ref, volt_hbm, start_hbm, gen_hbm, ann_hbm, grain_hbm, r3t_hbm, ky_ref,
    dens_hbm, src_ref,
    E, N0, N1, N2, GEN, ANN, GR, RD, BX, MX, BY, MY, BZ, MZ, B0, U0, HEAT, R3T, HZ, SEND, GOTL, GOTR,
    in_sem, out_sem, send_sem, recv_sem,
):
    X, Y, Z = GEN.shape
    me = lax.axis_index("slab")
    gy = lax.axis_index("gy")
    rows = slice(PAD, PAD + Y)
    chunks = range(0, Y, 8)
    t_rows = src_ref.shape[1]

    loads = {}

    def load(key, src, dst):
        copy = pltpu.make_async_copy(src, dst, in_sem.at[len(loads)])
        copy.start()
        loads[key] = copy

    inner = pl.ds(1, X - 2)
    for layer in (0, X - 1):
        load(("v", layer), volt_hbm.at[layer], E.at[layer + 1, pl.ds(PAD, Y)])
        load(("g", layer), grain_hbm.at[layer], GR.at[layer])
        load(("n", layer), start_hbm.at[layer], N0.at[layer + 1, pl.ds(PAD, Y)])
    load("v", volt_hbm.at[inner], E.at[pl.ds(2, X - 2), pl.ds(PAD, Y)])
    load("g", grain_hbm.at[inner], GR.at[inner])
    load("a", ann_hbm, ANN)
    load("n", start_hbm.at[inner], N0.at[pl.ds(2, X - 2), pl.ds(PAD, Y)])
    load("gen", gen_hbm, GEN)
    load("r3t", r3t_hbm, R3T)

    zero_rows = jnp.zeros((X + 2, PAD, Z), jnp.float32)
    zero_layer = jnp.zeros((Y, Z), jnp.float32)
    for buf in (E, N0, N1, N2):
        buf[:, 0:PAD, :] = zero_rows
        buf[:, PAD + Y:2 * PAD + Y, :] = zero_rows

        @pl.when(me == 0)
        def _():
            buf[0, rows, :] = zero_layer

        @pl.when(me == slabs - 1)
        def _():
            buf[X + 1, rows, :] = zero_layer

    @pl.when(me == 0)
    def _():
        GOTL[...] = jnp.zeros_like(GOTL)

    @pl.when(me == slabs - 1)
    def _():
        GOTR[...] = jnp.zeros_like(GOTR)

    x_sides = [(me > 0, (me - 1, gy)), (me < slabs - 1, (me + 1, gy))]
    y_sides = [] if yblocks == 1 else [(gy > 0, (me, gy - 1)), (gy < yblocks - 1, (me, gy + 1))]

    barrier = pltpu.get_barrier_semaphore()
    for has, device in x_sides + y_sides:
        @pl.when(has)
        def _():
            pl.semaphore_signal(barrier, inc=1, device_id=device, device_id_type=MESH)
    peers = sum(has.astype(jnp.int32) for has, _ in x_sides + y_sides)
    pl.semaphore_wait(barrier, peers)

    def side_copy(slot, d, device, src, dst):
        return pltpu.make_async_remote_copy(
            src_ref=src, dst_ref=dst, send_sem=send_sem.at[slot, d], recv_sem=recv_sem.at[slot, d],
            device_id=device, device_id_type=MESH,
        )

    def x_copies(slot, buf):
        body = pl.ds(PAD, Y)
        return [
            (has, side_copy(slot, d, device, buf.at[1 if d == 0 else X, body], buf.at[X + 1 if d == 0 else 0, body]))
            for d, (has, device) in enumerate(x_sides)
        ]

    def y_copies(slot, buf):
        layers = pl.ds(1, X)
        return [
            (has, side_copy(
                slot, 2 + d, device,
                buf.at[layers, pl.ds(PAD if d == 0 else Y, PAD)],
                buf.at[layers, pl.ds(PAD + Y if d == 0 else 0, PAD)],
            ))
            for d, (has, device) in enumerate(y_sides)
        ]

    def start(copies):
        for has, copy in copies:
            @pl.when(has)
            def _():
                copy.start()

    def finish(copies):
        for (has, copy), (_, mirror) in zip(copies, copies[::-1]):
            @pl.when(has)
            def _():
                copy.wait_send()
                mirror.wait_recv()

    def exchange_y(slot, buf):
        copies = y_copies(slot, buf)
        start(copies)
        finish(copies)

    def over_layers(first, last, body):
        def step(x, carry):
            body(x)
            return carry
        lax.fori_loop(first, last, step, 0)

    shifts = [shift_ref[g] for g in range(GRAINS)]

    def effective(x):
        for y in chunks:
            grain = GR[x, y:y + 8, :]
            shift = jnp.where(grain == 0, shifts[0], 0.0)
            for g in range(1, GRAINS):
                shift = jnp.where(grain == g, shifts[g], shift)
            E[x + 1, PAD + y:PAD + y + 8, :] = E[x + 1, PAD + y:PAD + y + 8, :] + shift

    for layer in (0, X - 1):
        loads[("v", layer)].wait()
        loads[("g", layer)].wait()
        effective(layer)
    e_copies = x_copies(0, E)
    start(e_copies)
    for layer in (0, X - 1):
        loads[("n", layer)].wait()
    n_copies = x_copies(1, N0)
    start(n_copies)
    loads["v"].wait()
    loads["g"].wait()
    over_layers(1, X - 1, effective)
    loads["n"].wait()
    if y_sides:
        exchange_y(0, E)
        exchange_y(1, N0)
    loads["a"].wait()

    lane = lax.broadcasted_iota(jnp.int32, (8, Z), 1)
    first_lane = lane == 0
    last_lane = lane == Z - 1
    lane0 = lax.broadcasted_iota(jnp.int32, (8, 128), 1) == 0

    def up_z(v):
        return jnp.where(last_lane, 0.0, pltpu.roll(v, Z - 1, 1))

    def down_z(v):
        return jnp.where(first_lane, 0.0, pltpu.roll(v, 1, 1))

    def yz_faces(x):
        u = E[x + 1, PAD:PAD + 8, :] - E[x + 1, PAD - 1:PAD + 7, :]
        b = bernoulli(u)
        BY[x, PAD - 1:PAD, :] = b[0:1]
        MY[x, PAD - 1:PAD, :] = b[0:1] + u[0:1]
        for y in chunks:
            r = PAD + y
            e = E[x + 1, r:r + 8, :]
            uy = E[x + 1, r + 1:r + 9, :] - e
            by = bernoulli(uy)
            my = by + uy
            BY[x, r:r + 8, :] = by
            MY[x, r:r + 8, :] = my
            uz = up_z(e) - e
            bz = bernoulli(uz)
            mz = bz + uz
            BZ[x, y:y + 8, :] = bz
            MZ[x, y:y + 8, :] = mz
            e0 = e[:, 0:128]
            b0 = bernoulli(e0)
            B0[x, y:y + 8, :] = jnp.where(lane0, b0, 0.0)
            U0[x, y:y + 8, :] = jnp.where(lane0, 0.5 * e0 * b0, 0.0)
            RD[x, y:y + 8, :] = ANN[x, y:y + 8, :] + my + mz + down_z(bz) + BY[x, r - 1:r + 7, :]
            RD[x, y:y + 8, 0:128] = RD[x, y:y + 8, 0:128] + B0[x, y:y + 8, :]

    over_layers(0, X, yz_faces)

    def x_face(f):
        for y in chunks:
            r = PAD + y
            u = E[f + 1, r:r + 8, :] - E[f, r:r + 8, :]
            b = bernoulli(u)
            BX[f, y:y + 8, :] = b
            MX[f, y:y + 8, :] = b + u

    over_layers(1, X, x_face)
    finish(e_copies)
    x_face(0)
    x_face(X)
    loads["gen"].wait()
    finish(n_copies)

    def sweep(src, dst, first):
        def layer(x):
            for y in chunks:
                r = PAD + y
                c = slice(y, y + 8)
                n = src[x + 1, r:r + 8, :]
                total = GEN[x, c, :] + BX[x + 1, c, :] * src[x + 2, r:r + 8, :] + MX[x, c, :] * src[x, r:r + 8, :]
                total = total + BY[x, r:r + 8, :] * src[x + 1, r + 1:r + 9, :]
                total = total + MY[x, r - 1:r + 7, :] * src[x + 1, r - 1:r + 7, :]
                total = total + BZ[x, c, :] * up_z(n) + down_z(MZ[x, c, :] * n)
                if first:
                    rd = 1.0 / (RD[x, c, :] + MX[x + 1, c, :] + BX[x, c, :])
                    RD[x, c, :] = rd
                else:
                    rd = RD[x, c, :]
                dst[x + 1, r:r + 8, :] = total * rd
        return layer

    first = sweep(N0, N1, True)
    over_layers(0, 1, first)
    over_layers(X - 1, X, first)
    one_copies = x_copies(2, N1)
    start(one_copies)
    over_layers(1, X - 1, first)
    if y_sides:
        exchange_y(2, N1)
    second = sweep(N1, N2, False)
    over_layers(1, X - 1, second)
    finish(one_copies)
    over_layers(0, 1, second)
    over_layers(X - 1, X, second)
    two_copies = x_copies(3, N2)
    start(two_copies)
    out = pltpu.make_async_copy(N2.at[pl.ds(1, X), pl.ds(PAD, Y)], dens_hbm, out_sem)
    out.start()
    if y_sides:
        exchange_y(3, N2)

    def heat(x):
        for y in chunks:
            r = PAD + y
            c = slice(y, y + 8)
            n = N2[x + 1, r:r + 8, :]

            def term(b, m, low, high):
                return (m - b) * (b * high - m * low)

            total = term(BX[x + 1, c, :], MX[x + 1, c, :], n, N2[x + 2, r:r + 8, :])
            total = total + term(BX[x, c, :], MX[x, c, :], N2[x, r:r + 8, :], n)
            total = total + term(BY[x, r:r + 8, :], MY[x, r:r + 8, :], n, N2[x + 1, r + 1:r + 9, :])
            total = total + term(
                BY[x, r - 1:r + 7, :], MY[x, r - 1:r + 7, :], N2[x + 1, r - 1:r + 7, :], n
            )
            fz = term(BZ[x, c, :], MZ[x, c, :], n, up_z(n))
            total = total + fz + down_z(fz)
            HEAT[x, c, :] = 0.5 * total
            HEAT[x, c, 0:128] = HEAT[x, c, 0:128] + U0[x, c, :] * n[:, 0:128]

    over_layers(1, X - 1, heat)
    finish(two_copies)
    over_layers(0, 1, heat)
    over_layers(X - 1, X, heat)

    loads["r3t"].wait()
    HZ[...] = jnp.dot(
        HEAT[...].reshape(X * Y, Z), R3T[...], precision=HIGHEST, preferred_element_type=jnp.float32
    ).reshape(HZ.shape)
    A = X // 2
    parts = []
    for a in range(A + 2):
        total = None
        for x in range(max(0, 2 * a - 3), min(X, 2 * a + 1)):
            piece = wx_ref[a, x] * HZ[x]
            total = piece if total is None else total + piece
        parts.append(total)
    share = jnp.dot(
        ky_ref[...], jnp.concatenate(parts, axis=0), precision=HIGHEST, preferred_element_type=jnp.float32
    )
    SEND[...] = share.reshape(SEND.shape)
    has_l, left = x_sides[0]
    has_r, right = x_sides[1]
    copies = [
        (has_l, side_copy(4, 0, left, SEND.at[pl.ds(0, A)], GOTR)),
        (has_r, side_copy(4, 1, right, SEND.at[pl.ds(2, A)], GOTL)),
    ]
    start(copies)
    finish(copies)
    src_ref[0:A - 2] = GOTL[0:A - 2]
    src_ref[A - 2] = GOTL[A - 2] + SEND[0]
    src_ref[A - 1] = GOTL[A - 1] + SEND[1]
    src_ref[A:2 * A - 2] = SEND[2:A]
    src_ref[2 * A - 2] = SEND[A] + GOTR[0]
    src_ref[2 * A - 1] = SEND[A + 1] + GOTR[1]
    src_ref[2 * A:] = GOTR[2:]
    out.wait()


def thermal_kernel(src_ref, start_ref, rc_ref, out_ref, ta, tb):
    A = out_ref.shape[0] - 2
    T, C = out_ref.shape[1:]
    row = lax.broadcasted_iota(jnp.int32, (T, C), 0)
    col = lax.broadcasted_iota(jnp.int32, (T, C), 1)
    bufs = [start_ref, ta, tb, None]
    width = start_ref.shape[0]
    for sweep in range(HEAT_SWEEPS):
        old = bufs[sweep]
        for a in range(sweep + 1, width - 1 - sweep):
            v = old[a]
            total = src_ref[a - 1] + old[a - 1] + old[a + 1]
            total = total + jnp.where(row == T - 1, 0.0, pltpu.roll(v, T - 1, 0))
            total = total + jnp.where(row == 0, 0.0, pltpu.roll(v, 1, 0))
            total = total + jnp.where(col == C - 1, 0.0, pltpu.roll(v, C - 1, 1))
            total = total + jnp.where(col == 0, 0.0, pltpu.roll(v, 1, 1))
            new = total * rc_ref[a]
            if sweep == HEAT_SWEEPS - 1:
                out_ref[a - HEAT_SWEEPS] = new
            else:
                bufs[sweep + 1][a] = new


def prolong_kernel(wx_ref, t_ref, ky_ref, r3_ref, out_ref, spread):
    X = wx_ref.shape[1]
    A = X // 2
    T, C = t_ref.shape[1:]

    @pl.when(pl.program_id(0) == 0)
    def _():
        for x in range(X):
            total = None
            for a in range(A + 2):
                if max(0, 2 * a - 3) <= x < 2 * a + 1:
                    piece = wx_ref[a, x] * t_ref[a]
                    total = piece if total is None else total + piece
            spread[x * T:(x + 1) * T, :] = total

    part = jnp.dot(ky_ref[...], spread[...], precision=HIGHEST, preferred_element_type=jnp.float32)
    out_ref[...] = jnp.dot(part, r3_ref[...], precision=HIGHEST, preferred_element_type=jnp.float32)


def per_device(
    volt, start, gen, ann, grain, barrier_shift, r1, r2, r3, cooling, warming,
):
    slabs, yblocks = lax.axis_size("slab"), lax.axis_size("gy")
    X, Y, Z = volt.shape
    C, T = r3.shape[0], r2.shape[0]
    CL, _, AT = warming.shape
    A = X // 2
    me = lax.axis_index("slab")
    f32 = jnp.float32

    wx = lax.dynamic_slice(jnp.pad(r1, ((1, 1), (0, 0))), (me * A, me * X), (A + 2, X))
    eye = jnp.eye(X, dtype=f32)
    ky = jnp.einsum("ij,tc->itjc", eye, r2, precision=HIGHEST).reshape(X * T, X * Y)

    both = jnp.stack([warming, 1.0 / (6.0 + cooling)]).reshape(2, CL * T, AT)
    both = jnp.pad(both.transpose(0, 2, 1), ((0, 0), (A, A), (0, 0))).reshape(2, slabs + 2, A, CL * T)
    both = jnp.concatenate([both[:, i:i + slabs] for i in range(3)], axis=2)
    both = both.transpose(1, 0, 2, 3).reshape(slabs, 6 * A, CL * T)
    both = lax.all_to_all(both, "slab", 0, 0, tiled=True)
    both = both.reshape(slabs, 6 * A, CL, T).transpose(1, 3, 0, 2).reshape(2, 3 * A, T, C)

    smem = pl.BlockSpec(memory_space=pltpu.SMEM)
    vmem = pl.BlockSpec(memory_space=pltpu.VMEM)
    anyspace = pl.BlockSpec(memory_space=pl.ANY)
    padded = pltpu.VMEM((X + 2, Y + 2 * PAD, Z), f32)
    block = pltpu.VMEM((X, Y, Z), f32)
    xface = pltpu.VMEM((X + 1, Y, Z), f32)
    yface = pltpu.VMEM((X, Y + PAD, Z), f32)
    edge = pltpu.VMEM((X, Y, 128), f32)
    cells = X * Y * Z
    density, source = pl.pallas_call(
        functools.partial(device_kernel, slabs, yblocks),
        out_shape=(
            jax.ShapeDtypeStruct((X, Y, Z), f32),
            jax.ShapeDtypeStruct((3 * A - 2, T, C), f32),
        ),
        in_specs=[smem, smem] + [anyspace] * 6 + [vmem],
        out_specs=(anyspace, vmem),
        scratch_shapes=[
            padded, padded, padded, padded, block, block, pltpu.VMEM((X, Y, Z), jnp.int32), block,
            xface, xface, yface, yface, block, block, edge, edge, block,
            pltpu.VMEM((Z, C), f32), pltpu.VMEM((X, Y, C), f32), pltpu.VMEM((A + 2, T, C), f32),
            pltpu.VMEM((A, T, C), f32), pltpu.VMEM((A, T, C), f32),
            pltpu.SemaphoreType.DMA((16,)), pltpu.SemaphoreType.DMA,
            pltpu.SemaphoreType.DMA((5, 4)), pltpu.SemaphoreType.DMA((5, 4)),
        ],
        compiler_params=pltpu.CompilerParams(
            collective_id=0, has_side_effects=True, vmem_limit_bytes=58 * MIB
        ),
        cost_estimate=pl.CostEstimate(flops=200 * cells, bytes_accessed=24 * cells, transcendentals=3 * cells),
    )(barrier_shift, wx, volt, start, gen, ann, grain, r3.T, ky[:(A + 2) * T, :(A + 2) * Y])

    if yblocks == 1:
        thermal = pl.pallas_call(
            thermal_kernel,
            out_shape=jax.ShapeDtypeStruct((A + 2, T, C), f32),
            in_specs=[vmem] * 3,
            out_specs=vmem,
            scratch_shapes=[pltpu.VMEM((3 * A, T, C), f32)] * 2,
        )(source, both[0], both[1])
    else:
        thermal = both[0]
        up = [(i, i + 1) for i in range(yblocks - 1)]
        down = [(i + 1, i) for i in range(yblocks - 1)]
        for sweep in range(HEAT_SWEEPS):
            low = lax.ppermute(thermal[:, -1:], "gy", up)
            high = lax.ppermute(thermal[:, :1], "gy", down)
            tall = jnp.concatenate([low, thermal, high], axis=1)
            wide = jnp.pad(thermal, ((0, 0), (0, 0), (1, 1)))
            total = source[sweep:3 * A - 2 - sweep] + thermal[2:] + thermal[:-2]
            total = total + (tall[:, 2:] + tall[:, :-2] + wide[:, :, 2:] + wide[:, :, :-2])[1:-1]
            thermal = total * both[1][sweep + 1:3 * A - 1 - sweep]

    mine = thermal[1:A + 1].reshape(A, T, slabs, CL).transpose(2, 0, 3, 1).reshape(slabs, A, CL * T)
    mine = lax.all_to_all(mine, "slab", 0, 0, tiled=True).reshape(AT, CL * T)
    thermal_out = mine.T.reshape(CL, T, AT)

    steps = 4
    fine = pl.pallas_call(
        prolong_kernel,
        grid=(steps,),
        out_shape=jax.ShapeDtypeStruct((X * Y, Z), f32),
        in_specs=[
            smem, vmem,
            pl.BlockSpec((X * Y // steps, X * T), lambda i: (i, 0)),
            vmem,
        ],
        out_specs=pl.BlockSpec((X * Y // steps, Z), lambda i: (i, 0)),
        scratch_shapes=[pltpu.VMEM((X * T, C), f32)],
        compiler_params=pltpu.CompilerParams(vmem_limit_bytes=24 * MIB),
        cost_estimate=pl.CostEstimate(
            flops=12 * X * Y * C * (X * T + Z), bytes_accessed=4 * (cells + C * Z), transcendentals=0
        ),
    )(wx, thermal, 16.0 * ky.T, r3)
    return density, thermal_out, fine.reshape(X, Y, Z)


def solution(mesh):
    cells = P("slab", "gy", None)
    in_specs = (cells,) * 5 + (P(), P(), P("gy", None), P(), cells, cells)
    return jax.shard_map(per_device, mesh=mesh, in_specs=in_specs, out_specs=(cells,) * 3, check_vma=False)
```

```python
import functools

import jax
import jax.numpy as jnp
from jax import lax
from jax.experimental import pallas as pl
from jax.experimental.pallas import tpu as pltpu
from jax.sharding import PartitionSpec as P

MESH = pl.DeviceIdType.MESH
HIGHEST = lax.Precision.HIGHEST
GRAINS = 4
HEAT_SWEEPS = 3
PAD = 8
MIB = 1024 * 1024


def inverse(v):
    r = pl.reciprocal(v, approx=True)
    return r * (2.0 - v * r)


def bernoulli(u):
    small = jnp.abs(u) < 0.03125
    series = 1.0 + u * (u * (1.0 / 12.0) - 0.5)
    return jnp.where(small, series, u * inverse(jnp.exp(u) - 1.0))


def product(a, b, dims=((1,), (0,))):
    return lax.dot_general(a, b, (dims, ((), ())), precision=HIGHEST, preferred_element_type=jnp.float32)


def device_kernel(
    slabs, yblocks,
    shift_ref, volt_hbm, start_hbm, gen_hbm, ann_hbm, grain_hbm, r3_hbm, *rest
):
    count = 4 if yblocks == 1 else 2
    extra_in, rest = rest[:count], rest[count:]
    count = 3 if yblocks == 1 else 2
    (dens_hbm, *extra_out), rest = rest[:count], rest[count:]
    (E, N0, N1, N2, GEN, ANN, GR, RD, BX, MX, BY, MY, BZ, MZ, B0, U0, HEAT, R3,
     in_sem, out_sem, send_sem, recv_sem, *extra) = rest
    X, Y, Z = GEN.shape
    me = lax.axis_index("slab")
    gy = lax.axis_index("gy")
    rows = slice(PAD, PAD + Y)
    chunks = range(0, Y, 8)

    loads = {}

    def load(key, src, dst):
        copy = pltpu.make_async_copy(src, dst, in_sem.at[len(loads)])
        copy.start()
        loads[key] = copy

    inner = pl.ds(1, X - 2)
    for layer in (0, X - 1):
        load(("v", layer), volt_hbm.at[layer], E.at[layer + 1, pl.ds(PAD, Y)])
        load(("g", layer), grain_hbm.at[layer], GR.at[layer])
        load(("n", layer), start_hbm.at[layer], N0.at[layer + 1, pl.ds(PAD, Y)])
    load("v", volt_hbm.at[inner], E.at[pl.ds(2, X - 2), pl.ds(PAD, Y)])
    load("g", grain_hbm.at[inner], GR.at[inner])
    load("a", ann_hbm, ANN)
    load("n", start_hbm.at[inner], N0.at[pl.ds(2, X - 2), pl.ds(PAD, Y)])
    load("gen", gen_hbm, GEN)
    load("r3", r3_hbm, R3)

    zero_rows = jnp.zeros((X + 2, PAD, Z), jnp.float32)
    zero_layer = jnp.zeros((Y, Z), jnp.float32)
    for buf in (E, N0, N1, N2):
        buf[:, 0:PAD, :] = zero_rows
        buf[:, PAD + Y:2 * PAD + Y, :] = zero_rows

        @pl.when(me == 0)
        def _():
            buf[0, rows, :] = zero_layer

        @pl.when(me == slabs - 1)
        def _():
            buf[X + 1, rows, :] = zero_layer

    def others(body):
        def step(i, carry):
            body(lax.rem(me + i, slabs))
            return carry
        lax.fori_loop(1, slabs, step, 0)

    if yblocks == 1:
        warm_ref, cool_ref, r2_tile, wx_rows = extra_in
        fine_hbm, thermal_ref = extra_out
        P, TRC, TR, SRC, W, SL, SR, GOTL, GOTR, OWN, RCV, all_send, all_recv = extra
        CL, T, AT = warm_ref.shape
        A = AT // slabs
        AW = A * T
        group = 128 // T
        low, mid, high = slice(0, AW), slice(AW, 2 * AW), slice(2 * AW, 3 * AW)

        for k in range(2):
            for c0 in range(0, CL, group):
                v = (warm_ref if k == 0 else cool_ref)[c0:c0 + group].reshape(group * T, AT)
                TR[...] = (v if k == 0 else 1.0 / (6.0 + v)).T
                cols = [TR[pl.ds(j, slabs, stride=A), :] for j in range(A)]
                for c in range(group):
                    P[k, pl.ds(c0 + c, slabs, stride=CL), :] = jnp.concatenate(
                        [v[:, c * T:(c + 1) * T] for v in cols], axis=1
                    )

        def slab_rows(d):
            return pl.ds(pl.multiple_of(d * CL, CL), CL)

        TRC[:, slab_rows(me), mid] = P[:, slab_rows(me), :]

        @pl.when(me == 0)
        def _():
            GOTL[...] = jnp.zeros_like(GOTL)
            TRC[:, :, low] = jnp.zeros((2, CL * slabs, AW), jnp.float32)

        @pl.when(me == slabs - 1)
        def _():
            GOTR[...] = jnp.zeros_like(GOTR)
            TRC[:, :, high] = jnp.zeros((2, CL * slabs, AW), jnp.float32)
    else:
        SEND, HZ, GOTL, GOTR = extra
        wx_ref, ky_ref = extra_in

        @pl.when(me == 0)
        def _():
            GOTL[...] = jnp.zeros_like(GOTL)

        @pl.when(me == slabs - 1)
        def _():
            GOTR[...] = jnp.zeros_like(GOTR)

    x_sides = [(me > 0, (me - 1, gy)), (me < slabs - 1, (me + 1, gy))]
    y_sides = [] if yblocks == 1 else [(gy > 0, (me, gy - 1)), (gy < yblocks - 1, (me, gy + 1))]

    barrier = pltpu.get_barrier_semaphore()
    if yblocks == 1:
        others(lambda d: pl.semaphore_signal(barrier, inc=1, device_id=(d, gy), device_id_type=MESH))
        pl.semaphore_wait(barrier, slabs - 1)
    else:
        for has, device in x_sides + y_sides:
            @pl.when(has)
            def _():
                pl.semaphore_signal(barrier, inc=1, device_id=device, device_id_type=MESH)
        peers = sum(has.astype(jnp.int32) for has, _ in x_sides + y_sides)
        pl.semaphore_wait(barrier, peers)

    def side_copy(slot, d, device, src, dst):
        return pltpu.make_async_remote_copy(
            src_ref=src, dst_ref=dst, send_sem=send_sem.at[slot, d], recv_sem=recv_sem.at[slot, d],
            device_id=device, device_id_type=MESH,
        )

    def x_copies(slot, buf):
        body = pl.ds(PAD, Y)
        return [
            (has, side_copy(slot, d, device, buf.at[1 if d == 0 else X, body], buf.at[X + 1 if d == 0 else 0, body]))
            for d, (has, device) in enumerate(x_sides)
        ]

    def y_copies(slot, buf):
        layers = pl.ds(1, X)
        return [
            (has, side_copy(
                slot, 2 + d, device,
                buf.at[layers, pl.ds(PAD if d == 0 else Y, PAD)],
                buf.at[layers, pl.ds(PAD + Y if d == 0 else 0, PAD)],
            ))
            for d, (has, device) in enumerate(y_sides)
        ]

    def start(copies):
        for has, copy in copies:
            @pl.when(has)
            def _():
                copy.start()

    def finish(copies):
        for (has, copy), (_, mirror) in zip(copies, copies[::-1]):
            @pl.when(has)
            def _():
                copy.wait_send()
                mirror.wait_recv()

    def exchange_y(slot, buf):
        copies = y_copies(slot, buf)
        start(copies)
        finish(copies)

    def over_layers(first, last, body):
        def step(x, carry):
            body(x)
            return carry
        lax.fori_loop(first, last, step, 0)

    shifts = [shift_ref[g] for g in range(GRAINS)]

    def effective(x):
        for y in chunks:
            grain = GR[x, y:y + 8, :]
            shift = jnp.where(grain == 0, shifts[0], 0.0)
            for g in range(1, GRAINS):
                shift = jnp.where(grain == g, shifts[g], shift)
            E[x + 1, PAD + y:PAD + y + 8, :] = E[x + 1, PAD + y:PAD + y + 8, :] + shift

    for layer in (0, X - 1):
        loads[("v", layer)].wait()
        loads[("g", layer)].wait()
        effective(layer)
    e_copies = x_copies(0, E)
    start(e_copies)
    for layer in (0, X - 1):
        loads[("n", layer)].wait()
    n_copies = x_copies(1, N0)
    start(n_copies)

    def all_copy(k, src, dst, d, s):
        return pltpu.make_async_remote_copy(
            src_ref=src, dst_ref=dst, send_sem=all_send.at[k, d], recv_sem=all_recv.at[k, s],
            device_id=(d, gy), device_id_type=MESH,
        )

    if yblocks == 1:
        def spread_copy(d, s):
            return all_copy(0, P.at[:, slab_rows(d)], TRC.at[:, slab_rows(s), pl.ds(AW, AW)], d, s)

        others(lambda d: spread_copy(d, me).start())
    loads["v"].wait()
    loads["g"].wait()
    over_layers(1, X - 1, effective)
    loads["n"].wait()
    if y_sides:
        exchange_y(0, E)
        exchange_y(1, N0)
    loads["a"].wait()

    lane = lax.broadcasted_iota(jnp.int32, (8, Z), 1)
    last_lane = lane == Z - 1
    edge = lax.broadcasted_iota(jnp.int32, (8, 128), 1)
    lane0, lane1 = edge == 0, edge == 127
    head, tail = slice(0, 128), slice(Z - 128, Z)

    def up_z(v):
        return pltpu.roll(v, Z - 1, 1)

    def down_z(v):
        return pltpu.roll(v, 1, 1)

    def yz_faces(x):
        u = E[x + 1, PAD:PAD + 8, :] - E[x + 1, PAD - 1:PAD + 7, :]
        b = bernoulli(u)
        BY[x, PAD - 1:PAD, :] = b[0:1]
        MY[x, PAD - 1:PAD, :] = b[0:1] + u[0:1]
        for y in chunks:
            r = PAD + y
            e = E[x + 1, r:r + 8, :]
            uy = E[x + 1, r + 1:r + 9, :] - e
            by = bernoulli(uy)
            my = by + uy
            BY[x, r:r + 8, :] = by
            MY[x, r:r + 8, :] = my
            uz = up_z(e) - e
            bz = bernoulli(uz)
            mz = jnp.where(last_lane, 0.0, bz + uz)
            bz = jnp.where(last_lane, 0.0, bz)
            BZ[x, y:y + 8, :] = bz
            MZ[x, y:y + 8, :] = mz
            e0 = jnp.where(lane0, e[:, head], e[:, tail])
            b0 = bernoulli(e0)
            U0[x, y:y + 8, :] = 0.5 * e0 * b0
            total = ANN[x, y:y + 8, :] + my + mz + down_z(bz) + BY[x, r - 1:r + 7, :]
            RD[x, y:y + 8, :] = total
            RD[x, y:y + 8, head] = total[:, head] + jnp.where(lane0, b0, 0.0)
            RD[x, y:y + 8, tail] = total[:, tail] + jnp.where(lane1, b0, 0.0)

    over_layers(0, X, yz_faces)

    def x_face(f):
        for y in chunks:
            r = PAD + y
            u = E[f + 1, r:r + 8, :] - E[f, r:r + 8, :]
            b = bernoulli(u)
            BX[f, y:y + 8, :] = b
            MX[f, y:y + 8, :] = b + u

    over_layers(1, X, x_face)
    finish(e_copies)
    x_face(0)
    x_face(X)
    loads["gen"].wait()
    finish(n_copies)
    if yblocks == 1:
        others(lambda s: spread_copy(s, s).wait_recv())
        block_copies = [
            (has, side_copy(5, d, device, TRC.at[:, :, pl.ds(AW, AW)], TRC.at[:, :, pl.ds(2 * AW if d == 0 else 0, AW)]))
            for d, (has, device) in enumerate(x_sides)
        ]

    def sweep(src, dst, first):
        def layer(x):
            for y in chunks:
                r = PAD + y
                c = slice(y, y + 8)
                n = src[x + 1, r:r + 8, :]
                total = GEN[x, c, :] + BX[x + 1, c, :] * src[x + 2, r:r + 8, :] + MX[x, c, :] * src[x, r:r + 8, :]
                total = total + BY[x, r:r + 8, :] * src[x + 1, r + 1:r + 9, :]
                total = total + MY[x, r - 1:r + 7, :] * src[x + 1, r - 1:r + 7, :]
                total = total + BZ[x, c, :] * up_z(n) + down_z(MZ[x, c, :] * n)
                if first:
                    rd = inverse(RD[x, c, :] + MX[x + 1, c, :] + BX[x, c, :])
                    RD[x, c, :] = rd
                else:
                    rd = RD[x, c, :]
                dst[x + 1, r:r + 8, :] = total * rd
        return layer

    first = sweep(N0, N1, True)
    over_layers(0, 1, first)
    over_layers(X - 1, X, first)
    one_copies = x_copies(2, N1)
    start(one_copies)
    if yblocks == 1:
        start(block_copies)
    over_layers(1, X - 1, first)
    if y_sides:
        exchange_y(2, N1)
    second = sweep(N1, N2, False)
    over_layers(1, X - 1, second)
    finish(one_copies)
    over_layers(0, 1, second)
    over_layers(X - 1, X, second)
    two_copies = x_copies(3, N2)
    start(two_copies)
    out = pltpu.make_async_copy(N2.at[pl.ds(1, X), pl.ds(PAD, Y)], dens_hbm, out_sem)
    out.start()
    if y_sides:
        exchange_y(3, N2)

    def solve_and_prolong():
        for x in range(X):
            W[x * Y:(x + 1) * Y, :] = r2_tile[...] * wx_rows[x:x + 1, :]
        along_z = product(R3[...], HEAT[...].reshape(X * Y, Z), ((1,), (1,)))
        SL[...] = product(along_z, W[:, AW - T:2 * AW - T])
        SR[...] = product(along_z, W[:, AW + T:2 * AW + T])
        copies = [
            (has, side_copy(4, d, device, SL if d == 0 else SR, GOTR if d == 0 else GOTL))
            for d, (has, device) in enumerate(x_sides)
        ]
        start(copies)

        def zeros(columns):
            return jnp.zeros((CL * slabs, columns * T), jnp.float32)

        SRC[...] = jnp.concatenate([zeros(A - 1), SL[...], zeros(A + 1)], axis=1)
        SRC[:, 2 * AW - T:2 * AW + T] = SRC[:, 2 * AW - T:2 * AW + T] + SR[:, AW - 2 * T:]
        finish(copies)
        SRC[...] = (
            SRC[...] + jnp.concatenate([zeros(1), GOTL[...], zeros(2 * A - 1)], axis=1)
            + jnp.concatenate([zeros(2 * A - 1), GOTR[...], zeros(1)], axis=1)
        )
        C = CL * slabs
        row = lax.broadcasted_iota(jnp.int32, (C, 3 * AW), 0)
        cell = lax.rem(lax.broadcasted_iota(jnp.int32, (C, 3 * AW), 1), T)
        for _ in range(HEAT_SWEEPS):
            v = TRC[0]
            total = SRC[...] + pltpu.roll(v, T, 1) + pltpu.roll(v, 3 * AW - T, 1)
            total = total + jnp.where(row == 0, 0.0, pltpu.roll(v, 1, 0))
            total = total + jnp.where(row == C - 1, 0.0, pltpu.roll(v, C - 1, 0))
            total = total + jnp.where(cell == 0, 0.0, pltpu.roll(v, 1, 1))
            total = total + jnp.where(cell == T - 1, 0.0, pltpu.roll(v, 3 * AW - 1, 1))
            TRC[0] = total * TRC[1]
        OWN[...] = TRC[0, :, mid]

        def back_copy(d, s):
            return all_copy(1, OWN.at[slab_rows(d)], RCV.at[slab_rows(s)], d, s)

        others(lambda d: back_copy(d, me).start())
        RCV[slab_rows(me), :] = OWN[slab_rows(me), :]
        spread = 16.0 * product(W[:, AW - T:2 * AW + T], TRC[0, :, AW - T:2 * AW + T], ((1,), (1,)))
        writes = []
        for x in range(0, X, 2):
            HEAT[x:x + 2] = product(spread[x * Y:(x + 2) * Y], R3[...]).reshape(2, Y, Z)
            writes.append(pltpu.make_async_copy(
                HEAT.at[pl.ds(x, 2)], fine_hbm.at[pl.ds(x, 2)], in_sem.at[len(loads) + len(writes)]
            ))
            writes[-1].start()
        others(lambda s: back_copy(s, s).wait_recv())
        for c0 in range(0, CL, group):
            cols = [RCV[pl.ds(c0 + c, slabs, stride=CL), :] for c in range(group)]
            for j in range(A):
                TR[pl.ds(j, slabs, stride=A), :] = jnp.concatenate(
                    [v[:, j * T:(j + 1) * T] for v in cols], axis=1
                )
            thermal_ref[c0:c0 + group] = TR[...].T.reshape(group, T, AT)
        others(lambda d: back_copy(d, me).wait_send())
        for write in writes:
            write.wait()

    def heat(x):
        for y in chunks:
            r = PAD + y
            c = slice(y, y + 8)
            n = N2[x + 1, r:r + 8, :]

            def term(b, m, low, high):
                return (m - b) * (b * high - m * low)

            total = term(BX[x + 1, c, :], MX[x + 1, c, :], n, N2[x + 2, r:r + 8, :])
            total = total + term(BX[x, c, :], MX[x, c, :], N2[x, r:r + 8, :], n)
            total = total + term(BY[x, r:r + 8, :], MY[x, r:r + 8, :], n, N2[x + 1, r + 1:r + 9, :])
            total = total + term(
                BY[x, r - 1:r + 7, :], MY[x, r - 1:r + 7, :], N2[x + 1, r - 1:r + 7, :], n
            )
            fz = term(BZ[x, c, :], MZ[x, c, :], n, up_z(n))
            total = total + fz + down_z(fz)
            total = 0.5 * total
            HEAT[x, c, :] = total
            u0 = U0[x, c, :]
            HEAT[x, c, head] = total[:, head] + jnp.where(lane0, u0 * n[:, head], 0.0)
            HEAT[x, c, tail] = total[:, tail] + jnp.where(lane1, u0 * n[:, tail], 0.0)

    over_layers(1, X - 1, heat)
    finish(two_copies)
    over_layers(0, 1, heat)
    over_layers(X - 1, X, heat)

    loads["r3"].wait()
    if yblocks == 1:
        finish(block_copies)
        others(lambda d: spread_copy(d, me).wait_send())
        solve_and_prolong()
        out.wait()
        return
    HZ[...] = product(HEAT[...].reshape(X * Y, Z), R3[...], ((1,), (1,))).reshape(HZ.shape)
    A = X // 2
    parts = []
    for a in range(A + 2):
        total = None
        for x in range(max(0, 2 * a - 3), min(X, 2 * a + 1)):
            piece = wx_ref[a, x] * HZ[x]
            total = piece if total is None else total + piece
        parts.append(total)
    share = jnp.dot(
        ky_ref[...], jnp.concatenate(parts, axis=0), precision=HIGHEST, preferred_element_type=jnp.float32
    )
    SEND[...] = share.reshape(SEND.shape)
    has_l, left = x_sides[0]
    has_r, right = x_sides[1]
    src_ref, = extra_out
    copies = [
        (has_l, side_copy(4, 0, left, SEND.at[pl.ds(0, A)], GOTR)),
        (has_r, side_copy(4, 1, right, SEND.at[pl.ds(2, A)], GOTL)),
    ]
    start(copies)
    finish(copies)
    src_ref[0:A - 2] = GOTL[0:A - 2]
    src_ref[A - 2] = GOTL[A - 2] + SEND[0]
    src_ref[A - 1] = GOTL[A - 1] + SEND[1]
    src_ref[A:2 * A - 2] = SEND[2:A]
    src_ref[2 * A - 2] = SEND[A] + GOTR[0]
    src_ref[2 * A - 1] = SEND[A + 1] + GOTR[1]
    src_ref[2 * A:] = GOTR[2:]
    out.wait()


def prolong_kernel(wx_ref, t_ref, ky_ref, r3_ref, out_ref, spread):
    X = wx_ref.shape[1]
    A = X // 2
    T, C = t_ref.shape[1:]

    @pl.when(pl.program_id(0) == 0)
    def _():
        for x in range(X):
            total = None
            for a in range(A + 2):
                if max(0, 2 * a - 3) <= x < 2 * a + 1:
                    piece = wx_ref[a, x] * t_ref[a]
                    total = piece if total is None else total + piece
            spread[x * T:(x + 1) * T, :] = total

    part = jnp.dot(ky_ref[...], spread[...], precision=HIGHEST, preferred_element_type=jnp.float32)
    out_ref[...] = jnp.dot(part, r3_ref[...], precision=HIGHEST, preferred_element_type=jnp.float32)


def per_device(
    volt, start, gen, ann, grain, barrier_shift, r1, r2, r3, cooling, warming,
):
    slabs, yblocks = lax.axis_size("slab"), lax.axis_size("gy")
    X, Y, Z = volt.shape
    C, T = r3.shape[0], r2.shape[0]
    CL, _, AT = warming.shape
    A = X // 2
    me = lax.axis_index("slab")
    f32 = jnp.float32

    wx = lax.dynamic_slice(jnp.pad(r1, ((1, 1), (0, 0))), (me * A, me * X), (A + 2, X))
    smem = pl.BlockSpec(memory_space=pltpu.SMEM)
    vmem = pl.BlockSpec(memory_space=pltpu.VMEM)
    anyspace = pl.BlockSpec(memory_space=pl.ANY)
    padded = pltpu.VMEM((X + 2, Y + 2 * PAD, Z), f32)
    block = pltpu.VMEM((X, Y, Z), f32)
    xface = pltpu.VMEM((X + 1, Y, Z), f32)
    yface = pltpu.VMEM((X, Y + PAD, Z), f32)
    edge = pltpu.VMEM((X, Y, 128), f32)
    cells = X * Y * Z
    scratch = [
        padded, padded, padded, padded, block, block, pltpu.VMEM((X, Y, Z), jnp.int32), block,
        xface, xface, yface, yface, block, block, edge, edge, block, pltpu.VMEM((C, Z), f32),
        pltpu.SemaphoreType.DMA((20,)), pltpu.SemaphoreType.DMA,
        pltpu.SemaphoreType.DMA((6, 4)), pltpu.SemaphoreType.DMA((6, 4)),
    ]
    full = jax.ShapeDtypeStruct((X, Y, Z), f32)
    call = functools.partial(
        pl.pallas_call,
        functools.partial(device_kernel, slabs, yblocks),
        compiler_params=pltpu.CompilerParams(
            collective_id=0, has_side_effects=True, vmem_limit_bytes=58 * MIB
        ),
        cost_estimate=pl.CostEstimate(flops=200 * cells, bytes_accessed=28 * cells, transcendentals=3 * cells),
    )
    operands = (barrier_shift, volt, start, gen, ann, grain, r3)

    if yblocks == 1:
        AW = A * T
        wx_rows = jnp.pad(wx.T, ((0, 0), (A - 1, A - 1)))
        wx_rows = jnp.repeat(wx_rows, T, axis=1)
        density, fine, thermal_out = call(
            out_shape=(full, full, jax.ShapeDtypeStruct((CL, T, AT), f32)),
            in_specs=[smem] + [anyspace] * 6 + [vmem] * 4,
            out_specs=(anyspace, anyspace, vmem),
            scratch_shapes=scratch + [
                pltpu.VMEM((2, C, AW), f32), pltpu.VMEM((2, C, 3 * AW), f32), pltpu.VMEM((AT, 128), f32),
                pltpu.VMEM((C, 3 * AW), f32), pltpu.VMEM((X * Y, 3 * AW), f32),
            ] + [pltpu.VMEM((C, AW), f32)] * 6 + [pltpu.SemaphoreType.DMA((2, slabs))] * 2,
        )(*operands, warming, cooling, jnp.tile(r2.T, (1, 3 * A)), wx_rows)
        return density, thermal_out, fine

    eye = jnp.eye(X, dtype=f32)
    ky = jnp.einsum("ij,tc->itjc", eye, r2, precision=HIGHEST).reshape(X * T, X * Y)
    both = jnp.stack([warming, 1.0 / (6.0 + cooling)]).reshape(2, CL * T, AT)
    both = jnp.pad(both.transpose(0, 2, 1), ((0, 0), (A, A), (0, 0))).reshape(2, slabs + 2, A, CL * T)
    both = jnp.concatenate([both[:, i:i + slabs] for i in range(3)], axis=2)
    both = both.transpose(1, 0, 2, 3).reshape(slabs, 6 * A, CL * T)
    both = lax.all_to_all(both, "slab", 0, 0, tiled=True)
    both = both.reshape(slabs, 6 * A, CL, T).transpose(1, 3, 0, 2).reshape(2, 3 * A, T, C)

    density, source = call(
        out_shape=(full, jax.ShapeDtypeStruct((3 * A - 2, T, C), f32)),
        in_specs=[smem] + [anyspace] * 6 + [smem, vmem],
        out_specs=(anyspace, vmem),
        scratch_shapes=scratch + [
            pltpu.VMEM((A + 2, T, C), f32), pltpu.VMEM((X, Y, C), f32),
            pltpu.VMEM((A, T, C), f32), pltpu.VMEM((A, T, C), f32),
        ],
    )(*operands, wx, ky[:(A + 2) * T, :(A + 2) * Y])

    thermal = both[0]
    up = [(i, i + 1) for i in range(yblocks - 1)]
    down = [(i + 1, i) for i in range(yblocks - 1)]
    for sweep in range(HEAT_SWEEPS):
        low = lax.ppermute(thermal[:, -1:], "gy", up)
        high = lax.ppermute(thermal[:, :1], "gy", down)
        tall = jnp.concatenate([low, thermal, high], axis=1)
        wide = jnp.pad(thermal, ((0, 0), (0, 0), (1, 1)))
        total = source[sweep:3 * A - 2 - sweep] + thermal[2:] + thermal[:-2]
        total = total + (tall[:, 2:] + tall[:, :-2] + wide[:, :, 2:] + wide[:, :, :-2])[1:-1]
        thermal = total * both[1][sweep + 1:3 * A - 1 - sweep]

    mine = thermal[1:A + 1].reshape(A, T, slabs, CL).transpose(2, 0, 3, 1).reshape(slabs, A, CL * T)
    mine = lax.all_to_all(mine, "slab", 0, 0, tiled=True).reshape(AT, CL * T)
    thermal_out = mine.T.reshape(CL, T, AT)

    steps = 4
    fine = pl.pallas_call(
        prolong_kernel,
        grid=(steps,),
        out_shape=jax.ShapeDtypeStruct((X * Y, Z), f32),
        in_specs=[
            smem, vmem,
            pl.BlockSpec((X * Y // steps, X * T), lambda i: (i, 0)),
            vmem,
        ],
        out_specs=pl.BlockSpec((X * Y // steps, Z), lambda i: (i, 0)),
        scratch_shapes=[pltpu.VMEM((X * T, C), f32)],
        compiler_params=pltpu.CompilerParams(vmem_limit_bytes=24 * MIB),
        cost_estimate=pl.CostEstimate(
            flops=12 * X * Y * C * (X * T + Z), bytes_accessed=4 * (cells + C * Z), transcendentals=0
        ),
    )(wx, thermal, 16.0 * ky.T, r3)
    return density, thermal_out, fine.reshape(X, Y, Z)


def solution(mesh):
    cells = P("slab", "gy", None)
    in_specs = (cells,) * 5 + (P(), P(), P("gy", None), P(), cells, cells)
    return jax.shard_map(per_device, mesh=mesh, in_specs=in_specs, out_specs=(cells,) * 3, check_vma=False)
```

```python
import functools

import jax
import jax.numpy as jnp
from jax import lax
from jax.experimental import pallas as pl
from jax.experimental.pallas import tpu as pltpu
from jax.sharding import PartitionSpec as P

MESH = pl.DeviceIdType.MESH
HIGHEST = lax.Precision.HIGHEST
GRAINS = 4
HEAT_SWEEPS = 3
PAD = 8
MIB = 1024 * 1024


def inverse(v):
    r = pl.reciprocal(v, approx=True)
    return r * (2.0 - v * r)


def bernoulli(u):
    small = jnp.abs(u) < 0.03125
    series = 1.0 + u * (u * (1.0 / 12.0) - 0.5)
    return jnp.where(small, series, u * inverse(jnp.exp(u) - 1.0))


def product(a, b, dims=((1,), (0,))):
    return lax.dot_general(a, b, (dims, ((), ())), precision=HIGHEST, preferred_element_type=jnp.float32)


def device_kernel(
    slabs, yblocks,
    shift_ref, volt_hbm, start_hbm, gen_hbm, ann_hbm, grain_hbm, r3_hbm, *rest
):
    count = 4 if yblocks == 1 else 2
    extra_in, rest = rest[:count], rest[count:]
    count = 3 if yblocks == 1 else 2
    (dens_hbm, *extra_out), rest = rest[:count], rest[count:]
    (E, N0, N1, N2, GEN, ANN, GR, RD, BX, MX, BY, MY, BZ, MZ, U0, HEAT, R3,
     in_sem, out_sem, send_sem, recv_sem, *extra) = rest
    X, Y, Z = GEN.shape
    me = lax.axis_index("slab")
    gy = lax.axis_index("gy")
    rows = slice(PAD, PAD + Y)

    loads = {}

    def load(key, src, dst):
        copy = pltpu.make_async_copy(src, dst, in_sem.at[len(loads)])
        copy.start()
        loads[key] = copy

    inner = pl.ds(1, X - 2)
    for layer in (0, X - 1):
        load(("v", layer), volt_hbm.at[layer], E.at[layer + 1, pl.ds(PAD, Y)])
        load(("g", layer), grain_hbm.at[layer], GR.at[layer])
        load(("n", layer), start_hbm.at[layer], N0.at[layer + 1, pl.ds(PAD, Y)])
    load("v", volt_hbm.at[inner], E.at[pl.ds(2, X - 2), pl.ds(PAD, Y)])
    load("g", grain_hbm.at[inner], GR.at[inner])
    load("a", ann_hbm, ANN)
    load("n", start_hbm.at[inner], N0.at[pl.ds(2, X - 2), pl.ds(PAD, Y)])
    load("gen", gen_hbm, GEN)
    load("r3", r3_hbm, R3)

    zero_rows = jnp.zeros((X + 2, PAD, Z), jnp.float32)
    zero_layer = jnp.zeros((Y, Z), jnp.float32)
    for buf in (E, N0, N1, N2):
        buf[:, 0:PAD, :] = zero_rows
        buf[:, PAD + Y:2 * PAD + Y, :] = zero_rows

        @pl.when(me == 0)
        def _():
            buf[0, rows, :] = zero_layer

        @pl.when(me == slabs - 1)
        def _():
            buf[X + 1, rows, :] = zero_layer

    barrier = pltpu.get_barrier_semaphore()

    def others(body):
        def step(i, carry):
            body(lax.rem(me + i, slabs))
            return carry
        lax.fori_loop(1, slabs, step, 0)

    if yblocks == 1:
        warm_ref, cool_ref, r1_ref, r2_ref = extra_in
        spread_ref, RCV = extra_out
        P, TRC, TR, SRC, W, SL, SR, GOTL, GOTR, OWN, LAND, all_send, all_recv = extra
        CL, T, AT = warm_ref.shape
        A = AT // slabs
        AW = A * T
        group = 128 // T
        others_rows = CL * (slabs - 1)
        low, mid, high = slice(0, AW), slice(AW, 2 * AW), slice(2 * AW, 3 * AW)

        @pl.when(me == 0)
        def _():
            GOTL[...] = jnp.zeros_like(GOTL)
            TRC[:, :, low] = jnp.zeros((2, CL * slabs, AW), jnp.float32)

        @pl.when(me == slabs - 1)
        def _():
            GOTR[...] = jnp.zeros_like(GOTR)
            TRC[:, :, high] = jnp.zeros((2, CL * slabs, AW), jnp.float32)
        others(lambda d: pl.semaphore_signal(barrier, inc=1, device_id=(d, gy), device_id_type=MESH))

        place = lax.broadcasted_iota
        pick_x = place(jnp.int32, (X, slabs * X), 1) == me * X + place(jnp.int32, (X, slabs * X), 0)
        pick_a = place(jnp.int32, (AT, 3 * AW), 0) == me * A - A + place(jnp.int32, (AT, 3 * AW), 1) // T
        wx_rows = product(pick_x.astype(jnp.float32), r1_ref[...], ((1,), (1,)))
        wx_rows = product(wx_rows, pick_a.astype(jnp.float32))
        r2_tile = jnp.concatenate([r2_ref[...].T] * (3 * A), axis=1)
        for x in range(X):
            W[x * Y:(x + 1) * Y, :] = r2_tile * wx_rows[x:x + 1, :]

        for k in range(2):
            for c0 in range(0, CL, group):
                v = (warm_ref if k == 0 else cool_ref)[c0:c0 + group].reshape(group * T, AT)
                TR[...] = (v if k == 0 else 1.0 / (6.0 + v)).T
                cols = [TR[pl.ds(j, slabs, stride=A), :] for j in range(A)]
                for c in range(group):
                    P[k, pl.ds(c0 + c, slabs, stride=CL), :] = jnp.concatenate(
                        [v[:, c * T:(c + 1) * T] for v in cols], axis=1
                    )

        def slab_rows(d):
            return pl.ds(pl.multiple_of(d * CL, CL), CL)

        TRC[:, slab_rows(me), mid] = P[:, slab_rows(me), :]
        pl.semaphore_wait(barrier, slabs - 1)

    else:
        SEND, HZ, GOTL, GOTR = extra
        wx_ref, ky_ref = extra_in

        @pl.when(me == 0)
        def _():
            GOTL[...] = jnp.zeros_like(GOTL)

        @pl.when(me == slabs - 1)
        def _():
            GOTR[...] = jnp.zeros_like(GOTR)

    x_sides = [(me > 0, (me - 1, gy)), (me < slabs - 1, (me + 1, gy))]
    y_sides = [] if yblocks == 1 else [(gy > 0, (me, gy - 1)), (gy < yblocks - 1, (me, gy + 1))]

    if yblocks > 1:
        for has, device in x_sides + y_sides:
            @pl.when(has)
            def _():
                pl.semaphore_signal(barrier, inc=1, device_id=device, device_id_type=MESH)
        peers = sum(has.astype(jnp.int32) for has, _ in x_sides + y_sides)
        pl.semaphore_wait(barrier, peers)

    def side_copy(slot, d, device, src, dst):
        return pltpu.make_async_remote_copy(
            src_ref=src, dst_ref=dst, send_sem=send_sem.at[slot, d], recv_sem=recv_sem.at[slot, d],
            device_id=device, device_id_type=MESH,
        )

    def x_copies(slot, buf):
        body = pl.ds(PAD, Y)
        return [
            (has, side_copy(slot, d, device, buf.at[1 if d == 0 else X, body], buf.at[X + 1 if d == 0 else 0, body]))
            for d, (has, device) in enumerate(x_sides)
        ]

    def y_copies(slot, buf):
        layers = pl.ds(1, X)
        return [
            (has, side_copy(
                slot, 2 + d, device,
                buf.at[layers, pl.ds(PAD if d == 0 else Y, PAD)],
                buf.at[layers, pl.ds(PAD + Y if d == 0 else 0, PAD)],
            ))
            for d, (has, device) in enumerate(y_sides)
        ]

    def start(copies):
        for has, copy in copies:
            @pl.when(has)
            def _():
                copy.start()

    def finish(copies):
        for (has, copy), (_, mirror) in zip(copies, copies[::-1]):
            @pl.when(has)
            def _():
                copy.wait_send()
                mirror.wait_recv()

    def exchange_y(slot, buf):
        copies = y_copies(slot, buf)
        start(copies)
        finish(copies)

    def over_layers(count, layer_of, body, at=None, action=None):
        def step(i, carry):
            if at is not None:
                pl.when(i == at)(action)
            body(layer_of(i))
            return carry
        lax.fori_loop(0, count, step, 0)

    def over_chunks(body, init=0):
        lax.fori_loop(0, Y // 8, lambda k, carry: body(pl.multiple_of(k * 8, 8), carry), init, unroll=2)

    def ends_first(i):
        return jnp.where(i == 0, 0, jnp.where(i == 1, X - 1, i - 1))

    def ends_last(i):
        return jnp.where(i < X - 2, i + 1, jnp.where(i == X - 2, 0, X - 1))

    row8 = lax.broadcasted_iota(jnp.int32, (8, Z), 0)

    def up_y(v, following):
        return pltpu.roll(jnp.where(row8 == 0, following, v), 7, 0)

    def down_y(v, preceding):
        return pltpu.roll(jnp.where(row8 == 7, preceding, v), 1, 0)

    shifts = [shift_ref[g] for g in range(GRAINS)]

    def effective(x):
        def chunk(y, carry):
            c, r = pl.ds(y, 8), pl.ds(y + PAD, 8)
            grain = GR[x, c, :]
            shift = jnp.where(grain == 0, shifts[0], 0.0)
            for g in range(1, GRAINS):
                shift = jnp.where(grain == g, shifts[g], shift)
            E[x + 1, r, :] = E[x + 1, r, :] + shift
            return carry
        over_chunks(chunk)

    for layer in (0, X - 1):
        loads[("v", layer)].wait()
        loads[("g", layer)].wait()
    over_layers(2, lambda i: i * (X - 1), effective)
    e_copies = x_copies(0, E)
    start(e_copies)
    for layer in (0, X - 1):
        loads[("n", layer)].wait()
    n_copies = x_copies(1, N0)
    start(n_copies)

    def all_copy(k, src, dst, d, s):
        return pltpu.make_async_remote_copy(
            src_ref=src, dst_ref=dst, send_sem=all_send.at[k], recv_sem=all_recv.at[k],
            device_id=(d, gy), device_id_type=MESH,
        )

    def wait_all(k, sem, ref):
        pltpu.make_async_copy(ref, ref, sem.at[k]).wait()

    if yblocks == 1:
        def spread_copy(d, s):
            return all_copy(0, P.at[:, slab_rows(d)], TRC.at[:, slab_rows(s), pl.ds(AW, AW)], d, s)

        others(lambda d: spread_copy(d, me).start())
    loads["v"].wait()
    loads["g"].wait()
    over_layers(X - 2, lambda i: i + 1, effective)
    loads["n"].wait()
    if y_sides:
        exchange_y(0, E)
        exchange_y(1, N0)
    loads["a"].wait()

    lane = lax.broadcasted_iota(jnp.int32, (8, Z), 1)
    last_lane = lane == Z - 1
    edge = lax.broadcasted_iota(jnp.int32, (8, 128), 1)
    lane0, lane1 = edge == 0, edge == 127
    head, tail = slice(0, 128), slice(Z - 128, Z)

    def up_z(v):
        return pltpu.roll(v, Z - 1, 1)

    def down_z(v):
        return pltpu.roll(v, 1, 1)

    def yz_faces(x):
        e = E[x + 1, 0:PAD, :]
        u = up_y(e, E[x + 1, PAD:PAD + 8, :]) - e
        b = bernoulli(u)
        BY[x, 0:PAD, :] = b
        MY[x, 0:PAD, :] = b + u

        def chunk(y, below):
            c, r = pl.ds(y, 8), pl.ds(y + PAD, 8)
            e = E[x + 1, r, :]
            uy = up_y(e, E[x + 1, pl.ds(y + PAD + 8, 8), :]) - e
            by = bernoulli(uy)
            my = by + uy
            BY[x, r, :] = by
            MY[x, r, :] = my
            uz = up_z(e) - e
            bz = bernoulli(uz)
            mz = jnp.where(last_lane, 0.0, bz + uz)
            bz = jnp.where(last_lane, 0.0, bz)
            BZ[x, c, :] = bz
            MZ[x, c, :] = mz
            e0 = jnp.where(lane0, e[:, head], e[:, tail])
            b0 = bernoulli(e0)
            U0[x, c, :] = 0.5 * e0 * b0
            total = ANN[x, c, :] + my + mz + down_z(bz) + down_y(by, below)
            RD[x, c, :] = total
            RD[x, c, head] = total[:, head] + jnp.where(lane0, b0, 0.0)
            RD[x, c, tail] = total[:, tail] + jnp.where(lane1, b0, 0.0)
            return by
        over_chunks(chunk, b)

    over_layers(X, lambda i: i, yz_faces)

    def x_face(f):
        def chunk(y, carry):
            c, r = pl.ds(y, 8), pl.ds(y + PAD, 8)
            u = E[f + 1, r, :] - E[f, r, :]
            b = bernoulli(u)
            BX[f, c, :] = b
            MX[f, c, :] = b + u
            return carry
        over_chunks(chunk)

    over_layers(
        X + 1, lambda i: jnp.where(i < X - 1, i + 1, (i - (X - 1)) * X), x_face, X - 1, lambda: finish(e_copies)
    )
    loads["gen"].wait()
    finish(n_copies)
    if yblocks == 1:
        wait_all(0, all_recv, TRC.at[:, pl.ds(0, others_rows), pl.ds(AW, AW)])
        block_copies = [
            (has, side_copy(5, d, device, TRC.at[:, :, pl.ds(AW, AW)], TRC.at[:, :, pl.ds(2 * AW if d == 0 else 0, AW)]))
            for d, (has, device) in enumerate(x_sides)
        ]

    def sweep(src, dst, first):
        def layer(x):
            def chunk(y, below):
                c, r = pl.ds(y, 8), pl.ds(y + PAD, 8)
                n = src[x + 1, r, :]
                total = GEN[x, c, :] + BX[x + 1, c, :] * src[x + 2, r, :] + MX[x, c, :] * src[x, r, :]
                total = total + BY[x, r, :] * up_y(n, src[x + 1, pl.ds(y + PAD + 8, 8), :])
                product_y = MY[x, r, :] * n
                total = total + down_y(product_y, below)
                total = total + BZ[x, c, :] * up_z(n) + down_z(MZ[x, c, :] * n)
                if first:
                    rd = inverse(RD[x, c, :] + MX[x + 1, c, :] + BX[x, c, :])
                    RD[x, c, :] = rd
                else:
                    rd = RD[x, c, :]
                dst[x + 1, r, :] = total * rd
                return product_y
            over_chunks(chunk, MY[x, 0:PAD, :] * src[x + 1, 0:PAD, :])
        return layer

    one_copies = x_copies(2, N1)

    def send_one():
        start(one_copies)
        if yblocks == 1:
            start(block_copies)

    over_layers(X, ends_first, sweep(N0, N1, True), 2, send_one)
    if y_sides:
        exchange_y(2, N1)
    over_layers(X, ends_last, sweep(N1, N2, False), X - 2, lambda: finish(one_copies))
    two_copies = x_copies(3, N2)
    start(two_copies)
    out = pltpu.make_async_copy(N2.at[pl.ds(1, X), pl.ds(PAD, Y)], dens_hbm, out_sem)
    out.start()
    if y_sides:
        exchange_y(3, N2)

    def solve_and_prolong():
        along_z = product(R3[...], HEAT[...].reshape(X * Y, Z), ((1,), (1,)))
        SL[...] = product(along_z, W[:, AW - T:2 * AW - T])
        SR[...] = product(along_z, W[:, AW + T:2 * AW + T])
        copies = [
            (has, side_copy(4, d, device, SL if d == 0 else SR, GOTR if d == 0 else GOTL))
            for d, (has, device) in enumerate(x_sides)
        ]
        start(copies)

        def zeros(columns):
            return jnp.zeros((CL * slabs, columns * T), jnp.float32)

        SRC[...] = jnp.concatenate([zeros(A - 1), SL[...], zeros(A + 1)], axis=1)
        SRC[:, 2 * AW - T:2 * AW + T] = SRC[:, 2 * AW - T:2 * AW + T] + SR[:, AW - 2 * T:]
        finish(copies)
        SRC[...] = (
            SRC[...] + jnp.concatenate([zeros(1), GOTL[...], zeros(2 * A - 1)], axis=1)
            + jnp.concatenate([zeros(2 * A - 1), GOTR[...], zeros(1)], axis=1)
        )
        C = CL * slabs
        row = lax.broadcasted_iota(jnp.int32, (C, 3 * AW), 0)
        cell = lax.rem(lax.broadcasted_iota(jnp.int32, (C, 3 * AW), 1), T)
        for _ in range(HEAT_SWEEPS):
            v = TRC[0]
            total = SRC[...] + pltpu.roll(v, T, 1) + pltpu.roll(v, 3 * AW - T, 1)
            total = total + jnp.where(row == 0, 0.0, pltpu.roll(v, 1, 0))
            total = total + jnp.where(row == C - 1, 0.0, pltpu.roll(v, C - 1, 0))
            total = total + jnp.where(cell == 0, 0.0, pltpu.roll(v, 1, 1))
            total = total + jnp.where(cell == T - 1, 0.0, pltpu.roll(v, 3 * AW - 1, 1))
            TRC[0] = total * TRC[1]
        OWN[...] = TRC[0, :, mid]

        def back_copy(d, s):
            return all_copy(1, OWN.at[slab_rows(d)], LAND.at[slab_rows(s)], d, s)

        others(lambda d: back_copy(d, me).start())
        LAND[slab_rows(me), :] = OWN[slab_rows(me), :]
        spread_ref[...] = 16.0 * product(W[:, AW - T:2 * AW + T], TRC[0, :, AW - T:2 * AW + T], ((1,), (1,)))
        wait_all(1, all_recv, LAND.at[pl.ds(0, others_rows)])
        RCV[...] = LAND[...]
        wait_all(1, all_send, OWN.at[pl.ds(0, others_rows)])

    def heat(x):
        def term(b, m, low, high):
            return (m - b) * (b * high - m * low)

        def y_term(r, n, following):
            return term(BY[x, r, :], MY[x, r, :], n, up_y(n, following))

        def chunk(y, below):
            c, r = pl.ds(y, 8), pl.ds(y + PAD, 8)
            n = N2[x + 1, r, :]
            total = term(BX[x + 1, c, :], MX[x + 1, c, :], n, N2[x + 2, r, :])
            total = total + term(BX[x, c, :], MX[x, c, :], N2[x, r, :], n)
            fy = y_term(r, n, N2[x + 1, pl.ds(y + PAD + 8, 8), :])
            total = total + fy + down_y(fy, below)
            fz = term(BZ[x, c, :], MZ[x, c, :], n, up_z(n))
            total = 0.5 * (total + fz + down_z(fz))
            HEAT[x, c, :] = total
            u0 = U0[x, c, :]
            HEAT[x, c, head] = total[:, head] + jnp.where(lane0, u0 * n[:, head], 0.0)
            HEAT[x, c, tail] = total[:, tail] + jnp.where(lane1, u0 * n[:, tail], 0.0)
            return fy
        over_chunks(chunk, y_term(slice(0, PAD), N2[x + 1, 0:PAD, :], N2[x + 1, PAD:PAD + 8, :]))

    over_layers(X, ends_last, heat, X - 2, lambda: finish(two_copies))

    loads["r3"].wait()
    if yblocks == 1:
        finish(block_copies)
        wait_all(0, all_send, P.at[:, pl.ds(0, others_rows)])
        solve_and_prolong()
        out.wait()
        return
    HZ[...] = product(HEAT[...].reshape(X * Y, Z), R3[...], ((1,), (1,))).reshape(HZ.shape)
    A = X // 2
    parts = []
    for a in range(A + 2):
        total = None
        for x in range(max(0, 2 * a - 3), min(X, 2 * a + 1)):
            piece = wx_ref[a, x] * HZ[x]
            total = piece if total is None else total + piece
        parts.append(total)
    share = jnp.dot(
        ky_ref[...], jnp.concatenate(parts, axis=0), precision=HIGHEST, preferred_element_type=jnp.float32
    )
    SEND[...] = share.reshape(SEND.shape)
    has_l, left = x_sides[0]
    has_r, right = x_sides[1]
    src_ref, = extra_out
    copies = [
        (has_l, side_copy(4, 0, left, SEND.at[pl.ds(0, A)], GOTR)),
        (has_r, side_copy(4, 1, right, SEND.at[pl.ds(2, A)], GOTL)),
    ]
    start(copies)
    finish(copies)
    src_ref[0:A - 2] = GOTL[0:A - 2]
    src_ref[A - 2] = GOTL[A - 2] + SEND[0]
    src_ref[A - 1] = GOTL[A - 1] + SEND[1]
    src_ref[A:2 * A - 2] = SEND[2:A]
    src_ref[2 * A - 2] = SEND[A] + GOTR[0]
    src_ref[2 * A - 1] = SEND[A + 1] + GOTR[1]
    src_ref[2 * A:] = GOTR[2:]
    out.wait()


def finish_kernel(spread_ref, r3_ref, dens_ref, got_ref, fine_ref, dens_out, thermal_ref, tr):
    CL, T, AT = thermal_ref.shape
    A = got_ref.shape[1] // T
    slabs, group = AT // A, 128 // T
    dens_out[...] = dens_ref[...]
    fine_ref[...] = product(spread_ref[...], r3_ref[...]).reshape(fine_ref.shape)

    @pl.when(pl.program_id(0) == 0)
    def _():
        for c0 in range(0, CL, group):
            cols = [got_ref[pl.ds(c0 + c, slabs, stride=CL), :] for c in range(group)]
            for j in range(A):
                tr[pl.ds(j, slabs, stride=A), :] = jnp.concatenate(
                    [v[:, j * T:(j + 1) * T] for v in cols], axis=1
                )
            thermal_ref[c0:c0 + group] = tr[...].T.reshape(group, T, AT)


def prolong_kernel(wx_ref, t_ref, ky_ref, r3_ref, out_ref, spread):
    X = wx_ref.shape[1]
    A = X // 2
    T, C = t_ref.shape[1:]

    @pl.when(pl.program_id(0) == 0)
    def _():
        for x in range(X):
            total = None
            for a in range(A + 2):
                if max(0, 2 * a - 3) <= x < 2 * a + 1:
                    piece = wx_ref[a, x] * t_ref[a]
                    total = piece if total is None else total + piece
            spread[x * T:(x + 1) * T, :] = total

    part = jnp.dot(ky_ref[...], spread[...], precision=HIGHEST, preferred_element_type=jnp.float32)
    out_ref[...] = jnp.dot(part, r3_ref[...], precision=HIGHEST, preferred_element_type=jnp.float32)


def per_device(
    volt, start, gen, ann, grain, barrier_shift, r1, r2, r3, cooling, warming,
):
    slabs, yblocks = lax.axis_size("slab"), lax.axis_size("gy")
    X, Y, Z = volt.shape
    C, T = r3.shape[0], r2.shape[0]
    CL, _, AT = warming.shape
    A = X // 2
    me = lax.axis_index("slab")
    f32 = jnp.float32

    wx = lax.dynamic_slice(jnp.pad(r1, ((1, 1), (0, 0))), (me * A, me * X), (A + 2, X))
    smem = pl.BlockSpec(memory_space=pltpu.SMEM)
    vmem = pl.BlockSpec(memory_space=pltpu.VMEM)
    anyspace = pl.BlockSpec(memory_space=pl.ANY)
    padded = pltpu.VMEM((X + 2, Y + 2 * PAD, Z), f32)
    block = pltpu.VMEM((X, Y, Z), f32)
    xface = pltpu.VMEM((X + 1, Y, Z), f32)
    yface = pltpu.VMEM((X, Y + PAD, Z), f32)
    edge = pltpu.VMEM((X, Y, 128), f32)
    cells = X * Y * Z
    scratch = [
        padded, padded, padded, padded, block, block, pltpu.VMEM((X, Y, Z), jnp.int32), block,
        xface, xface, yface, yface, block, block, edge, block, pltpu.VMEM((C, Z), f32),
        pltpu.SemaphoreType.DMA((20,)), pltpu.SemaphoreType.DMA,
        pltpu.SemaphoreType.DMA((6, 4)), pltpu.SemaphoreType.DMA((6, 4)),
    ]
    full = jax.ShapeDtypeStruct((X, Y, Z), f32)
    call = functools.partial(
        pl.pallas_call,
        functools.partial(device_kernel, slabs, yblocks),
        compiler_params=pltpu.CompilerParams(
            collective_id=0, has_side_effects=True, vmem_limit_bytes=58 * MIB
        ),
        cost_estimate=pl.CostEstimate(flops=200 * cells, bytes_accessed=28 * cells, transcendentals=3 * cells),
    )
    operands = (barrier_shift, volt, start, gen, ann, grain, r3)

    if yblocks == 1:
        AW = A * T
        density, spread, got = call(
            out_shape=(
                full, jax.ShapeDtypeStruct((X * Y, C), f32), jax.ShapeDtypeStruct((C, AW), f32)
            ),
            in_specs=[smem] + [anyspace] * 6 + [vmem] * 4,
            out_specs=(anyspace, vmem, vmem),
            scratch_shapes=scratch + [
                pltpu.VMEM((2, C, AW), f32), pltpu.VMEM((2, C, 3 * AW), f32), pltpu.VMEM((AT, 128), f32),
                pltpu.VMEM((C, 3 * AW), f32), pltpu.VMEM((X * Y, 3 * AW), f32),
            ] + [pltpu.VMEM((C, AW), f32)] * 6 + [pltpu.SemaphoreType.DMA((2,))] * 2,
        )(*operands, warming, cooling, r1, r2)
        steps = X // 2
        layers = pl.BlockSpec((X // steps, Y, Z), lambda i: (i, 0, 0))
        fine, density, thermal_out = pl.pallas_call(
            finish_kernel,
            grid=(steps,),
            out_shape=(full, full, jax.ShapeDtypeStruct((CL, T, AT), f32)),
            in_specs=[
                pl.BlockSpec((X * Y // steps, C), lambda i: (i, 0)),
                pl.BlockSpec((C, Z), lambda i: (0, 0)),
                layers,
                pl.BlockSpec((C, AW), lambda i: (0, 0)),
            ],
            out_specs=(layers, layers, pl.BlockSpec((CL, T, AT), lambda i: (0, 0, 0))),
            scratch_shapes=[pltpu.VMEM((AT, 128), f32)],
            compiler_params=pltpu.CompilerParams(vmem_limit_bytes=24 * MIB),
            cost_estimate=pl.CostEstimate(
                flops=12 * X * Y * C * Z, bytes_accessed=4 * (3 * cells + C * Z), transcendentals=0
            ),
        )(spread, r3, density, got)
        return density, thermal_out, fine

    eye = jnp.eye(X, dtype=f32)
    ky = jnp.einsum("ij,tc->itjc", eye, r2, precision=HIGHEST).reshape(X * T, X * Y)
    both = jnp.stack([warming, 1.0 / (6.0 + cooling)]).reshape(2, CL * T, AT)
    both = jnp.pad(both.transpose(0, 2, 1), ((0, 0), (A, A), (0, 0))).reshape(2, slabs + 2, A, CL * T)
    both = jnp.concatenate([both[:, i:i + slabs] for i in range(3)], axis=2)
    both = both.transpose(1, 0, 2, 3).reshape(slabs, 6 * A, CL * T)
    both = lax.all_to_all(both, "slab", 0, 0, tiled=True)
    both = both.reshape(slabs, 6 * A, CL, T).transpose(1, 3, 0, 2).reshape(2, 3 * A, T, C)

    density, source = call(
        out_shape=(full, jax.ShapeDtypeStruct((3 * A - 2, T, C), f32)),
        in_specs=[smem] + [anyspace] * 6 + [smem, vmem],
        out_specs=(anyspace, vmem),
        scratch_shapes=scratch + [
            pltpu.VMEM((A + 2, T, C), f32), pltpu.VMEM((X, Y, C), f32),
            pltpu.VMEM((A, T, C), f32), pltpu.VMEM((A, T, C), f32),
        ],
    )(*operands, wx, ky[:(A + 2) * T, :(A + 2) * Y])

    thermal = both[0]
    up = [(i, i + 1) for i in range(yblocks - 1)]
    down = [(i + 1, i) for i in range(yblocks - 1)]
    for sweep in range(HEAT_SWEEPS):
        low = lax.ppermute(thermal[:, -1:], "gy", up)
        high = lax.ppermute(thermal[:, :1], "gy", down)
        tall = jnp.concatenate([low, thermal, high], axis=1)
        wide = jnp.pad(thermal, ((0, 0), (0, 0), (1, 1)))
        total = source[sweep:3 * A - 2 - sweep] + thermal[2:] + thermal[:-2]
        total = total + (tall[:, 2:] + tall[:, :-2] + wide[:, :, 2:] + wide[:, :, :-2])[1:-1]
        thermal = total * both[1][sweep + 1:3 * A - 1 - sweep]

    mine = thermal[1:A + 1].reshape(A, T, slabs, CL).transpose(2, 0, 3, 1).reshape(slabs, A, CL * T)
    mine = lax.all_to_all(mine, "slab", 0, 0, tiled=True).reshape(AT, CL * T)
    thermal_out = mine.T.reshape(CL, T, AT)

    steps = 4
    fine = pl.pallas_call(
        prolong_kernel,
        grid=(steps,),
        out_shape=jax.ShapeDtypeStruct((X * Y, Z), f32),
        in_specs=[
            smem, vmem,
            pl.BlockSpec((X * Y // steps, X * T), lambda i: (i, 0)),
            vmem,
        ],
        out_specs=pl.BlockSpec((X * Y // steps, Z), lambda i: (i, 0)),
        scratch_shapes=[pltpu.VMEM((X * T, C), f32)],
        compiler_params=pltpu.CompilerParams(vmem_limit_bytes=24 * MIB),
        cost_estimate=pl.CostEstimate(
            flops=12 * X * Y * C * (X * T + Z), bytes_accessed=4 * (cells + C * Z), transcendentals=0
        ),
    )(wx, thermal, 16.0 * ky.T, r3)
    return density, thermal_out, fine.reshape(X, Y, Z)


def solution(mesh):
    cells = P("slab", "gy", None)
    in_specs = (cells,) * 5 + (P(), P(), P("gy", None), P(), cells, cells)
    return jax.shard_map(per_device, mesh=mesh, in_specs=in_specs, out_specs=(cells,) * 3, check_vma=False)
```

```python
import functools

import jax
import jax.numpy as jnp
from jax import lax
from jax.experimental import pallas as pl
from jax.experimental.pallas import tpu as pltpu
from jax.sharding import PartitionSpec as P

MESH = pl.DeviceIdType.MESH
HIGHEST = lax.Precision.HIGHEST
GRAINS = 4
HEAT_SWEEPS = 3
PAD = 8
MIB = 1024 * 1024


def inverse(v):
    r = pl.reciprocal(v, approx=True)
    return r * (2.0 - v * r)


def bernoulli(u):
    small = jnp.abs(u) < 0.03125
    series = 1.0 + u * (u * (1.0 / 12.0) - 0.5)
    return jnp.where(small, series, u * inverse(jnp.exp(u) - 1.0))


def product(a, b, dims=((1,), (0,))):
    return lax.dot_general(a, b, (dims, ((), ())), precision=HIGHEST, preferred_element_type=jnp.float32)


def halves(v):
    high = v.astype(jnp.bfloat16)
    return high, (v - high.astype(jnp.float32)).astype(jnp.bfloat16)


def split_product(a, b, dims=((1,), (0,))):
    def dot(p, q):
        return lax.dot_general(p, q, (dims, ((), ())), preferred_element_type=jnp.float32)

    return dot(a[0], b[0]) + (dot(a[0], b[1]) + dot(a[1], b[0]))


def device_kernel(
    slabs, yblocks,
    shift_ref, volt_hbm, start_hbm, gen_hbm, ann_hbm, grain_hbm, r3_hbm, *rest
):
    count = 4 if yblocks == 1 else 2
    extra_in, rest = rest[:count], rest[count:]
    count = 3 if yblocks == 1 else 2
    (dens_hbm, *extra_out), rest = rest[:count], rest[count:]
    (E, N0, N1, N2, GEN, ANN, GR, RD, BX, MX, BY, MY, BZ, MZ, U0, HEAT, R3,
     in_sem, out_sem, send_sem, recv_sem, *extra) = rest
    X, Y, Z = GEN.shape
    me = lax.axis_index("slab")
    gy = lax.axis_index("gy")
    rows = slice(PAD, PAD + Y)

    loads = {}

    def load(key, src, dst):
        copy = pltpu.make_async_copy(src, dst, in_sem.at[len(loads)])
        copy.start()
        loads[key] = copy

    inner = pl.ds(1, X - 2)
    for layer in (0, X - 1):
        load(("v", layer), volt_hbm.at[layer], E.at[layer + 1, pl.ds(PAD, Y)])
        load(("g", layer), grain_hbm.at[layer], GR.at[layer])
        load(("n", layer), start_hbm.at[layer], N0.at[layer + 1, pl.ds(PAD, Y)])
    load("v", volt_hbm.at[inner], E.at[pl.ds(2, X - 2), pl.ds(PAD, Y)])
    load("g", grain_hbm.at[inner], GR.at[inner])
    load("a", ann_hbm, ANN)
    load("n", start_hbm.at[inner], N0.at[pl.ds(2, X - 2), pl.ds(PAD, Y)])
    load("gen", gen_hbm, GEN)
    load("r3", r3_hbm, R3)

    zero_rows = jnp.zeros((X + 2, PAD, Z), jnp.float32)
    zero_layer = jnp.zeros((Y, Z), jnp.float32)
    for buf in (E, N0, N1, N2):
        buf[:, 0:PAD, :] = zero_rows
        buf[:, PAD + Y:2 * PAD + Y, :] = zero_rows

        @pl.when(me == 0)
        def _():
            buf[0, rows, :] = zero_layer

        @pl.when(me == slabs - 1)
        def _():
            buf[X + 1, rows, :] = zero_layer

    barrier = pltpu.get_barrier_semaphore()

    def slot_of(x):
        return (x + X - 2) if x == 0 else (x if x == X - 1 else x - 1)

    def others(body):
        def step(i, carry):
            body(lax.rem(me + i, slabs))
            return carry
        lax.fori_loop(1, slabs, step, 0)

    if yblocks == 1:
        warm_ref, cool_ref, r1_ref, r2_ref = extra_in
        spread_ref, RCV = extra_out
        P, TRC, TR, SRC, WR, WP, SL, SR, GOTL, GOTR, OWN, LAND, all_send, all_recv = extra
        CL, T, AT = warm_ref.shape
        A = AT // slabs
        AW = A * T
        group = 128 // T
        others_rows = CL * (slabs - 1)
        low, mid, high = slice(0, AW), slice(AW, 2 * AW), slice(2 * AW, 3 * AW)

        @pl.when(me == 0)
        def _():
            GOTL[...] = jnp.zeros_like(GOTL)
            TRC[:, :, low] = jnp.zeros((2, CL * slabs, AW), jnp.float32)

        @pl.when(me == slabs - 1)
        def _():
            GOTR[...] = jnp.zeros_like(GOTR)
            TRC[:, :, high] = jnp.zeros((2, CL * slabs, AW), jnp.float32)
        others(lambda d: pl.semaphore_signal(barrier, inc=1, device_id=(d, gy), device_id_type=MESH))

        place = lax.broadcasted_iota
        pick_x = place(jnp.int32, (X, slabs * X), 1) == me * X + place(jnp.int32, (X, slabs * X), 0)
        pick_a = place(jnp.int32, (AT, 3 * AW), 0) == me * A - A + place(jnp.int32, (AT, 3 * AW), 1) // T
        wx_rows = product(pick_x.astype(jnp.float32), r1_ref[...], ((1,), (1,)))
        wx_rows = product(wx_rows, pick_a.astype(jnp.float32))
        r2_tile = jnp.concatenate([r2_ref[...].T] * (3 * A), axis=1)
        for x in range(X):
            rows_x = slice(slot_of(x) * Y, slot_of(x) * Y + Y)
            w = r2_tile * wx_rows[x:x + 1, :]
            w_left, w_right = w[:, AW - T:2 * AW - T], w[:, AW + T:2 * AW + T]
            for k, half in enumerate(halves(jnp.concatenate([w_left, w_right], axis=1))):
                WR[k, rows_x, :] = half
            for k, half in enumerate(halves(w[:, AW - T:2 * AW + T])):
                WP[k, rows_x, :] = half

        for k in range(2):
            for c0 in range(0, CL, group):
                v = (warm_ref if k == 0 else cool_ref)[c0:c0 + group].reshape(group * T, AT)
                TR[...] = (v if k == 0 else 1.0 / (6.0 + v)).T
                cols = [TR[pl.ds(j, slabs, stride=A), :] for j in range(A)]
                for c in range(group):
                    P[k, pl.ds(c0 + c, slabs, stride=CL), :] = jnp.concatenate(
                        [v[:, c * T:(c + 1) * T] for v in cols], axis=1
                    )

        def slab_rows(d):
            return pl.ds(pl.multiple_of(d * CL, CL), CL)

        TRC[:, slab_rows(me), mid] = P[:, slab_rows(me), :]
        pl.semaphore_wait(barrier, slabs - 1)

    else:
        SEND, HZ, GOTL, GOTR = extra
        wx_ref, ky_ref = extra_in

        @pl.when(me == 0)
        def _():
            GOTL[...] = jnp.zeros_like(GOTL)

        @pl.when(me == slabs - 1)
        def _():
            GOTR[...] = jnp.zeros_like(GOTR)

    x_sides = [(me > 0, (me - 1, gy)), (me < slabs - 1, (me + 1, gy))]
    y_sides = [] if yblocks == 1 else [(gy > 0, (me, gy - 1)), (gy < yblocks - 1, (me, gy + 1))]

    if yblocks > 1:
        for has, device in x_sides + y_sides:
            @pl.when(has)
            def _():
                pl.semaphore_signal(barrier, inc=1, device_id=device, device_id_type=MESH)
        peers = sum(has.astype(jnp.int32) for has, _ in x_sides + y_sides)
        pl.semaphore_wait(barrier, peers)

    def side_copy(slot, d, device, src, dst):
        return pltpu.make_async_remote_copy(
            src_ref=src, dst_ref=dst, send_sem=send_sem.at[slot, d], recv_sem=recv_sem.at[slot, d],
            device_id=device, device_id_type=MESH,
        )

    def x_copies(slot, buf):
        body = pl.ds(PAD, Y)
        return [
            (has, side_copy(slot, d, device, buf.at[1 if d == 0 else X, body], buf.at[X + 1 if d == 0 else 0, body]))
            for d, (has, device) in enumerate(x_sides)
        ]

    def y_copies(slot, buf):
        layers = pl.ds(1, X)
        return [
            (has, side_copy(
                slot, 2 + d, device,
                buf.at[layers, pl.ds(PAD if d == 0 else Y, PAD)],
                buf.at[layers, pl.ds(PAD + Y if d == 0 else 0, PAD)],
            ))
            for d, (has, device) in enumerate(y_sides)
        ]

    def start(copies):
        for has, copy in copies:
            @pl.when(has)
            def _():
                copy.start()

    def finish(copies):
        for (has, copy), (_, mirror) in zip(copies, copies[::-1]):
            @pl.when(has)
            def _():
                copy.wait_send()
                mirror.wait_recv()

    def exchange_y(slot, buf):
        copies = y_copies(slot, buf)
        start(copies)
        finish(copies)

    def over_layers(count, layer_of, body, at=None, action=None):
        def step(i, carry):
            if at is not None:
                pl.when(i == at)(action)
            body(layer_of(i))
            return carry
        lax.fori_loop(0, count, step, 0)

    def over_chunks(body, init=0):
        lax.fori_loop(0, Y // 8, lambda k, carry: body(pl.multiple_of(k * 8, 8), carry), init, unroll=2)

    def ends_first(i):
        return jnp.where(i == 0, 0, jnp.where(i == 1, X - 1, i - 1))

    def ends_last(i):
        return jnp.where(i < X - 2, i + 1, jnp.where(i == X - 2, 0, X - 1))

    row8 = lax.broadcasted_iota(jnp.int32, (8, Z), 0)

    def up_y(v, following):
        return pltpu.roll(jnp.where(row8 == 0, following, v), 7, 0)

    def down_y(v, preceding):
        return pltpu.roll(jnp.where(row8 == 7, preceding, v), 1, 0)

    shifts = [shift_ref[g] for g in range(GRAINS)]

    def effective(x):
        def chunk(y, carry):
            c, r = pl.ds(y, 8), pl.ds(y + PAD, 8)
            grain = GR[x, c, :]
            shift = jnp.where(grain == 0, shifts[0], 0.0)
            for g in range(1, GRAINS):
                shift = jnp.where(grain == g, shifts[g], shift)
            E[x + 1, r, :] = E[x + 1, r, :] + shift
            return carry
        over_chunks(chunk)

    for layer in (0, X - 1):
        loads[("v", layer)].wait()
        loads[("g", layer)].wait()
    over_layers(2, lambda i: i * (X - 1), effective)
    e_copies = x_copies(0, E)
    start(e_copies)
    for layer in (0, X - 1):
        loads[("n", layer)].wait()
    n_copies = x_copies(1, N0)
    start(n_copies)

    def all_copy(k, src, dst, d, s):
        return pltpu.make_async_remote_copy(
            src_ref=src, dst_ref=dst, send_sem=all_send.at[k], recv_sem=all_recv.at[k],
            device_id=(d, gy), device_id_type=MESH,
        )

    def wait_all(k, sem, ref):
        pltpu.make_async_copy(ref, ref, sem.at[k]).wait()

    if yblocks == 1:
        def spread_copy(d, s):
            return all_copy(0, P.at[:, slab_rows(d)], TRC.at[:, slab_rows(s), pl.ds(AW, AW)], d, s)

        others(lambda d: spread_copy(d, me).start())
    loads["v"].wait()
    loads["g"].wait()
    over_layers(X - 2, lambda i: i + 1, effective)
    loads["n"].wait()
    if y_sides:
        exchange_y(0, E)
        exchange_y(1, N0)
    loads["a"].wait()

    lane = lax.broadcasted_iota(jnp.int32, (8, Z), 1)
    last_lane = lane == Z - 1
    edge = lax.broadcasted_iota(jnp.int32, (8, 128), 1)
    lane0, lane1 = edge == 0, edge == 127
    head, tail = slice(0, 128), slice(Z - 128, Z)

    def up_z(v):
        return pltpu.roll(v, Z - 1, 1)

    def down_z(v):
        return pltpu.roll(v, 1, 1)

    def yz_faces(x):
        e = E[x + 1, 0:PAD, :]
        u = up_y(e, E[x + 1, PAD:PAD + 8, :]) - e
        b = bernoulli(u)
        BY[x, 0:PAD, :] = b
        MY[x, 0:PAD, :] = b + u

        def chunk(y, below):
            c, r = pl.ds(y, 8), pl.ds(y + PAD, 8)
            e = E[x + 1, r, :]
            uy = up_y(e, E[x + 1, pl.ds(y + PAD + 8, 8), :]) - e
            by = bernoulli(uy)
            my = by + uy
            BY[x, r, :] = by
            MY[x, r, :] = my
            uz = up_z(e) - e
            bz = bernoulli(uz)
            mz = jnp.where(last_lane, 0.0, bz + uz)
            bz = jnp.where(last_lane, 0.0, bz)
            BZ[x, c, :] = bz
            MZ[x, c, :] = mz
            e0 = jnp.where(lane0, e[:, head], e[:, tail])
            b0 = bernoulli(e0)
            U0[x, c, :] = 0.5 * e0 * b0
            total = ANN[x, c, :] + my + mz + down_z(bz) + down_y(by, below)
            RD[x, c, :] = total
            RD[x, c, head] = total[:, head] + jnp.where(lane0, b0, 0.0)
            RD[x, c, tail] = total[:, tail] + jnp.where(lane1, b0, 0.0)
            return by
        over_chunks(chunk, b)

    over_layers(X, lambda i: i, yz_faces)

    def x_face(f):
        def chunk(y, carry):
            c, r = pl.ds(y, 8), pl.ds(y + PAD, 8)
            u = E[f + 1, r, :] - E[f, r, :]
            b = bernoulli(u)
            BX[f, c, :] = b
            MX[f, c, :] = b + u
            return carry
        over_chunks(chunk)

    over_layers(
        X + 1, lambda i: jnp.where(i < X - 1, i + 1, (i - (X - 1)) * X), x_face, X - 1, lambda: finish(e_copies)
    )
    loads["gen"].wait()
    finish(n_copies)
    if yblocks == 1:
        wait_all(0, all_recv, TRC.at[:, pl.ds(0, others_rows), pl.ds(AW, AW)])
        block_copies = [
            (has, side_copy(5, d, device, TRC.at[:, :, pl.ds(AW, AW)], TRC.at[:, :, pl.ds(2 * AW if d == 0 else 0, AW)]))
            for d, (has, device) in enumerate(x_sides)
        ]

    def sweep(src, dst, first):
        def layer(x):
            def chunk(y, below):
                c, r = pl.ds(y, 8), pl.ds(y + PAD, 8)
                n = src[x + 1, r, :]
                total = GEN[x, c, :] + BX[x + 1, c, :] * src[x + 2, r, :] + MX[x, c, :] * src[x, r, :]
                total = total + BY[x, r, :] * up_y(n, src[x + 1, pl.ds(y + PAD + 8, 8), :])
                product_y = MY[x, r, :] * n
                total = total + down_y(product_y, below)
                total = total + BZ[x, c, :] * up_z(n) + down_z(MZ[x, c, :] * n)
                if first:
                    rd = inverse(RD[x, c, :] + MX[x + 1, c, :] + BX[x, c, :])
                    RD[x, c, :] = rd
                else:
                    rd = RD[x, c, :]
                dst[x + 1, r, :] = total * rd
                return product_y
            over_chunks(chunk, MY[x, 0:PAD, :] * src[x + 1, 0:PAD, :])
        return layer

    one_copies = x_copies(2, N1)

    def send_one():
        start(one_copies)
        if yblocks == 1:
            start(block_copies)

    over_layers(X, ends_first, sweep(N0, N1, True), 2, send_one)
    if y_sides:
        exchange_y(2, N1)
    over_layers(X, ends_last, sweep(N1, N2, False), X - 2, lambda: finish(one_copies))
    two_copies = x_copies(3, N2)
    start(two_copies)
    out = pltpu.make_async_copy(N2.at[pl.ds(1, X), pl.ds(PAD, Y)], dens_hbm, out_sem)
    out.start()
    if y_sides:
        exchange_y(3, N2)

    def solve_and_prolong(inner_z, ends_z):
        share = split_product(halves(inner_z), (WR[0, :inner_rows], WR[1, :inner_rows]))
        share = share + split_product(halves(ends_z), (WR[0, inner_rows:], WR[1, inner_rows:]))
        SL[...] = share[:, :AW]
        SR[...] = share[:, AW:]
        copies = [
            (has, side_copy(4, d, device, SL if d == 0 else SR, GOTR if d == 0 else GOTL))
            for d, (has, device) in enumerate(x_sides)
        ]
        start(copies)

        def zeros(columns):
            return jnp.zeros((CL * slabs, columns * T), jnp.float32)

        SRC[...] = jnp.concatenate([zeros(A - 1), SL[...], zeros(A + 1)], axis=1)
        SRC[:, 2 * AW - T:2 * AW + T] = SRC[:, 2 * AW - T:2 * AW + T] + SR[:, AW - 2 * T:]
        finish(copies)
        SRC[...] = (
            SRC[...] + jnp.concatenate([zeros(1), GOTL[...], zeros(2 * A - 1)], axis=1)
            + jnp.concatenate([zeros(2 * A - 1), GOTR[...], zeros(1)], axis=1)
        )
        C = CL * slabs
        row = lax.broadcasted_iota(jnp.int32, (C, 3 * AW), 0)
        cell = lax.rem(lax.broadcasted_iota(jnp.int32, (C, 3 * AW), 1), T)
        for _ in range(HEAT_SWEEPS):
            v = TRC[0]
            total = SRC[...] + pltpu.roll(v, T, 1) + pltpu.roll(v, 3 * AW - T, 1)
            total = total + jnp.where(row == 0, 0.0, pltpu.roll(v, 1, 0))
            total = total + jnp.where(row == C - 1, 0.0, pltpu.roll(v, C - 1, 0))
            total = total + jnp.where(cell == 0, 0.0, pltpu.roll(v, 1, 1))
            total = total + jnp.where(cell == T - 1, 0.0, pltpu.roll(v, 3 * AW - 1, 1))
            TRC[0] = total * TRC[1]
        OWN[...] = TRC[0, :, mid]

        def back_copy(d, s):
            return all_copy(1, OWN.at[slab_rows(d)], LAND.at[slab_rows(s)], d, s)

        others(lambda d: back_copy(d, me).start())
        LAND[slab_rows(me), :] = OWN[slab_rows(me), :]
        spread = 16.0 * split_product((WP[0], WP[1]), halves(TRC[0, :, AW - T:2 * AW + T]), ((1,), (1,)))
        for x in range(X):
            spread_ref[x * Y:(x + 1) * Y, :] = spread[slot_of(x) * Y:slot_of(x) * Y + Y]
        wait_all(1, all_recv, LAND.at[pl.ds(0, others_rows)])
        RCV[...] = LAND[...]
        wait_all(1, all_send, OWN.at[pl.ds(0, others_rows)])

    def heat(x):
        slot = jnp.where(x == 0, X - 2, jnp.where(x == X - 1, X - 1, x - 1)) if yblocks == 1 else x

        def term(b, m, low, high):
            return (m - b) * (b * high - m * low)

        def y_term(r, n, following):
            return term(BY[x, r, :], MY[x, r, :], n, up_y(n, following))

        def chunk(y, below):
            c, r = pl.ds(y, 8), pl.ds(y + PAD, 8)
            n = N2[x + 1, r, :]
            total = term(BX[x + 1, c, :], MX[x + 1, c, :], n, N2[x + 2, r, :])
            total = total + term(BX[x, c, :], MX[x, c, :], N2[x, r, :], n)
            fy = y_term(r, n, N2[x + 1, pl.ds(y + PAD + 8, 8), :])
            total = total + fy + down_y(fy, below)
            fz = term(BZ[x, c, :], MZ[x, c, :], n, up_z(n))
            total = 0.5 * (total + fz + down_z(fz))
            HEAT[slot, c, :] = total
            u0 = U0[x, c, :]
            HEAT[slot, c, head] = total[:, head] + jnp.where(lane0, u0 * n[:, head], 0.0)
            HEAT[slot, c, tail] = total[:, tail] + jnp.where(lane1, u0 * n[:, tail], 0.0)
            return fy
        over_chunks(chunk, y_term(slice(0, PAD), N2[x + 1, 0:PAD, :], N2[x + 1, PAD:PAD + 8, :]))

    inner_rows = (X - 2) * Y
    if yblocks == 1:
        over_layers(X - 2, lambda i: i + 1, heat)
        loads["r3"].wait()
        r3 = halves(R3[...])
        flat = halves(HEAT[0:X - 2].reshape(inner_rows, Z))
        inner_z = split_product(r3, flat, ((1,), (1,)))
        finish(two_copies)
        over_layers(2, lambda i: i * (X - 1), heat)
        flat = halves(HEAT[X - 2:].reshape(2 * Y, Z))
        ends_z = split_product(halves(R3[...]), flat, ((1,), (1,)))
        finish(block_copies)
        wait_all(0, all_send, P.at[:, pl.ds(0, others_rows)])
        solve_and_prolong(inner_z, ends_z)
        out.wait()
        return

    over_layers(X, ends_last, heat, X - 2, lambda: finish(two_copies))
    loads["r3"].wait()
    HZ[...] = product(HEAT[...].reshape(X * Y, Z), R3[...], ((1,), (1,))).reshape(HZ.shape)
    A = X // 2
    parts = []
    for a in range(A + 2):
        total = None
        for x in range(max(0, 2 * a - 3), min(X, 2 * a + 1)):
            piece = wx_ref[a, x] * HZ[x]
            total = piece if total is None else total + piece
        parts.append(total)
    share = jnp.dot(
        ky_ref[...], jnp.concatenate(parts, axis=0), precision=HIGHEST, preferred_element_type=jnp.float32
    )
    SEND[...] = share.reshape(SEND.shape)
    has_l, left = x_sides[0]
    has_r, right = x_sides[1]
    src_ref, = extra_out
    copies = [
        (has_l, side_copy(4, 0, left, SEND.at[pl.ds(0, A)], GOTR)),
        (has_r, side_copy(4, 1, right, SEND.at[pl.ds(2, A)], GOTL)),
    ]
    start(copies)
    finish(copies)
    src_ref[0:A - 2] = GOTL[0:A - 2]
    src_ref[A - 2] = GOTL[A - 2] + SEND[0]
    src_ref[A - 1] = GOTL[A - 1] + SEND[1]
    src_ref[A:2 * A - 2] = SEND[2:A]
    src_ref[2 * A - 2] = SEND[A] + GOTR[0]
    src_ref[2 * A - 1] = SEND[A + 1] + GOTR[1]
    src_ref[2 * A:] = GOTR[2:]
    out.wait()


def finish_kernel(spread_ref, r3_ref, dens_ref, got_ref, fine_ref, dens_out, thermal_ref, tr):
    CL, T, AT = thermal_ref.shape
    A = got_ref.shape[1] // T
    slabs, group = AT // A, 128 // T
    dens_out[...] = dens_ref[...]
    fine_ref[...] = split_product(halves(spread_ref[...]), halves(r3_ref[...])).reshape(fine_ref.shape)

    @pl.when(pl.program_id(0) == 0)
    def _():
        for c0 in range(0, CL, group):
            cols = [got_ref[pl.ds(c0 + c, slabs, stride=CL), :] for c in range(group)]
            for j in range(A):
                tr[pl.ds(j, slabs, stride=A), :] = jnp.concatenate(
                    [v[:, j * T:(j + 1) * T] for v in cols], axis=1
                )
            thermal_ref[c0:c0 + group] = tr[...].T.reshape(group, T, AT)


def prolong_kernel(wx_ref, t_ref, ky_ref, r3_ref, out_ref, spread):
    X = wx_ref.shape[1]
    A = X // 2
    T, C = t_ref.shape[1:]

    @pl.when(pl.program_id(0) == 0)
    def _():
        for x in range(X):
            total = None
            for a in range(A + 2):
                if max(0, 2 * a - 3) <= x < 2 * a + 1:
                    piece = wx_ref[a, x] * t_ref[a]
                    total = piece if total is None else total + piece
            spread[x * T:(x + 1) * T, :] = total

    part = jnp.dot(ky_ref[...], spread[...], precision=HIGHEST, preferred_element_type=jnp.float32)
    out_ref[...] = jnp.dot(part, r3_ref[...], precision=HIGHEST, preferred_element_type=jnp.float32)


def per_device(
    volt, start, gen, ann, grain, barrier_shift, r1, r2, r3, cooling, warming,
):
    slabs, yblocks = lax.axis_size("slab"), lax.axis_size("gy")
    X, Y, Z = volt.shape
    C, T = r3.shape[0], r2.shape[0]
    CL, _, AT = warming.shape
    A = X // 2
    me = lax.axis_index("slab")
    f32 = jnp.float32

    wx = lax.dynamic_slice(jnp.pad(r1, ((1, 1), (0, 0))), (me * A, me * X), (A + 2, X))
    smem = pl.BlockSpec(memory_space=pltpu.SMEM)
    vmem = pl.BlockSpec(memory_space=pltpu.VMEM)
    anyspace = pl.BlockSpec(memory_space=pl.ANY)
    padded = pltpu.VMEM((X + 2, Y + 2 * PAD, Z), f32)
    block = pltpu.VMEM((X, Y, Z), f32)
    xface = pltpu.VMEM((X + 1, Y, Z), f32)
    yface = pltpu.VMEM((X, Y + PAD, Z), f32)
    edge = pltpu.VMEM((X, Y, 128), f32)
    cells = X * Y * Z
    scratch = [
        padded, padded, padded, padded, block, block, pltpu.VMEM((X, Y, Z), jnp.int32), block,
        xface, xface, yface, yface, block, block, edge, block, pltpu.VMEM((C, Z), f32),
        pltpu.SemaphoreType.DMA((20,)), pltpu.SemaphoreType.DMA,
        pltpu.SemaphoreType.DMA((6, 4)), pltpu.SemaphoreType.DMA((6, 4)),
    ]
    full = jax.ShapeDtypeStruct((X, Y, Z), f32)
    call = functools.partial(
        pl.pallas_call,
        functools.partial(device_kernel, slabs, yblocks),
        compiler_params=pltpu.CompilerParams(
            collective_id=0, has_side_effects=True, vmem_limit_bytes=58 * MIB
        ),
        cost_estimate=pl.CostEstimate(flops=200 * cells, bytes_accessed=28 * cells, transcendentals=3 * cells),
    )
    operands = (barrier_shift, volt, start, gen, ann, grain, r3)

    if yblocks == 1:
        AW = A * T
        density, spread, got = call(
            out_shape=(
                full, jax.ShapeDtypeStruct((X * Y, C), f32), jax.ShapeDtypeStruct((C, AW), f32)
            ),
            in_specs=[smem] + [anyspace] * 6 + [vmem] * 4,
            out_specs=(anyspace, vmem, vmem),
            scratch_shapes=scratch + [
                pltpu.VMEM((2, C, AW), f32), pltpu.VMEM((2, C, 3 * AW), f32), pltpu.VMEM((AT, 128), f32),
                pltpu.VMEM((C, 3 * AW), f32), pltpu.VMEM((2, X * Y, 2 * AW), jnp.bfloat16),
                pltpu.VMEM((2, X * Y, AW + 2 * T), jnp.bfloat16),
            ] + [pltpu.VMEM((C, AW), f32)] * 6 + [pltpu.SemaphoreType.DMA((2,))] * 2,
        )(*operands, warming, cooling, r1, r2)
        steps = X // 2
        layers = pl.BlockSpec((X // steps, Y, Z), lambda i: (i, 0, 0))
        fine, density, thermal_out = pl.pallas_call(
            finish_kernel,
            grid=(steps,),
            out_shape=(full, full, jax.ShapeDtypeStruct((CL, T, AT), f32)),
            in_specs=[
                pl.BlockSpec((X * Y // steps, C), lambda i: (i, 0)),
                pl.BlockSpec((C, Z), lambda i: (0, 0)),
                layers,
                pl.BlockSpec((C, AW), lambda i: (0, 0)),
            ],
            out_specs=(layers, layers, pl.BlockSpec((CL, T, AT), lambda i: (0, 0, 0))),
            scratch_shapes=[pltpu.VMEM((AT, 128), f32)],
            compiler_params=pltpu.CompilerParams(vmem_limit_bytes=58 * MIB),
            cost_estimate=pl.CostEstimate(
                flops=12 * X * Y * C * Z, bytes_accessed=4 * (3 * cells + C * Z), transcendentals=0
            ),
        )(spread, r3, density, got)
        return density, thermal_out, fine

    eye = jnp.eye(X, dtype=f32)
    ky = jnp.einsum("ij,tc->itjc", eye, r2, precision=HIGHEST).reshape(X * T, X * Y)
    both = jnp.stack([warming, 1.0 / (6.0 + cooling)]).reshape(2, CL * T, AT)
    both = jnp.pad(both.transpose(0, 2, 1), ((0, 0), (A, A), (0, 0))).reshape(2, slabs + 2, A, CL * T)
    both = jnp.concatenate([both[:, i:i + slabs] for i in range(3)], axis=2)
    both = both.transpose(1, 0, 2, 3).reshape(slabs, 6 * A, CL * T)
    both = lax.all_to_all(both, "slab", 0, 0, tiled=True)
    both = both.reshape(slabs, 6 * A, CL, T).transpose(1, 3, 0, 2).reshape(2, 3 * A, T, C)

    density, source = call(
        out_shape=(full, jax.ShapeDtypeStruct((3 * A - 2, T, C), f32)),
        in_specs=[smem] + [anyspace] * 6 + [smem, vmem],
        out_specs=(anyspace, vmem),
        scratch_shapes=scratch + [
            pltpu.VMEM((A + 2, T, C), f32), pltpu.VMEM((X, Y, C), f32),
            pltpu.VMEM((A, T, C), f32), pltpu.VMEM((A, T, C), f32),
        ],
    )(*operands, wx, ky[:(A + 2) * T, :(A + 2) * Y])

    thermal = both[0]
    up = [(i, i + 1) for i in range(yblocks - 1)]
    down = [(i + 1, i) for i in range(yblocks - 1)]
    for sweep in range(HEAT_SWEEPS):
        low = lax.ppermute(thermal[:, -1:], "gy", up)
        high = lax.ppermute(thermal[:, :1], "gy", down)
        tall = jnp.concatenate([low, thermal, high], axis=1)
        wide = jnp.pad(thermal, ((0, 0), (0, 0), (1, 1)))
        total = source[sweep:3 * A - 2 - sweep] + thermal[2:] + thermal[:-2]
        total = total + (tall[:, 2:] + tall[:, :-2] + wide[:, :, 2:] + wide[:, :, :-2])[1:-1]
        thermal = total * both[1][sweep + 1:3 * A - 1 - sweep]

    mine = thermal[1:A + 1].reshape(A, T, slabs, CL).transpose(2, 0, 3, 1).reshape(slabs, A, CL * T)
    mine = lax.all_to_all(mine, "slab", 0, 0, tiled=True).reshape(AT, CL * T)
    thermal_out = mine.T.reshape(CL, T, AT)

    steps = 4
    fine = pl.pallas_call(
        prolong_kernel,
        grid=(steps,),
        out_shape=jax.ShapeDtypeStruct((X * Y, Z), f32),
        in_specs=[
            smem, vmem,
            pl.BlockSpec((X * Y // steps, X * T), lambda i: (i, 0)),
            vmem,
        ],
        out_specs=pl.BlockSpec((X * Y // steps, Z), lambda i: (i, 0)),
        scratch_shapes=[pltpu.VMEM((X * T, C), f32)],
        compiler_params=pltpu.CompilerParams(vmem_limit_bytes=24 * MIB),
        cost_estimate=pl.CostEstimate(
            flops=12 * X * Y * C * (X * T + Z), bytes_accessed=4 * (cells + C * Z), transcendentals=0
        ),
    )(wx, thermal, 16.0 * ky.T, r3)
    return density, thermal_out, fine.reshape(X, Y, Z)


def solution(mesh):
    cells = P("slab", "gy", None)
    in_specs = (cells,) * 5 + (P(), P(), P("gy", None), P(), cells, cells)
    return jax.shard_map(per_device, mesh=mesh, in_specs=in_specs, out_specs=(cells,) * 3, check_vma=False)
```
